32 devices in a mesh: dp: 4 (over z), ctx: 4 (over x, core), tensor: 2 (over y).
Axes of the slice: x: 2, y: 2, z: 4, core: 2. Of those that a mesh axis runs over, the one named last changes fastest.
Arguments:
- inputs: bfloat16 [8, 1024, 2048], P('dp', 'ctx', 'tensor'), may hold values from -6 to 6
- cotangent: bfloat16 [8, 1024, 2048], P('dp', 'ctx', 'tensor'), may hold values from -6 to 6
- lengths: int32 [8], replicated, may hold values from 512 to 1024, as said below
- deal_order: int32 [8], replicated, may hold values from 0 to 7, each once
- query_weight: bfloat16 [2048, 2048], P('ctx', 'tensor'), may hold values from -0.125 to 0.125
- key_weight: bfloat16 [2048, 512], P('ctx', 'tensor'), may hold values from -0.125 to 0.125
- value_weight: bfloat16 [2048, 512], P('ctx', 'tensor'), may hold values from -0.125 to 0.125
- output_weight: bfloat16 [2048, 2048], P('tensor', 'ctx'), may hold values from -2 to 2
- gate_weight: bfloat16 [2048, 8192], P('ctx', 'tensor'), may hold values from -0.125 to 0.125
- up_weight: bfloat16 [2048, 8192], P('ctx', 'tensor'), may hold values from -0.125 to 0.125
- down_weight: bfloat16 [8192, 2048], P('tensor', 'ctx'), may hold values from -0.0625 to 0.0625
- attention_gain: float32 [2048], P('tensor'), may hold values from 0.1 to 1.9
- feedforward_gain: float32 [2048], P('tensor'), may hold values from 0.1 to 1.9
Outputs:
- outputs: bfloat16 [8, 1024, 2048], P('dp', 'ctx', 'tensor')
- input_grad: bfloat16 [8, 1024, 2048], P('dp', 'ctx', 'tensor')
- query_grad: float32 [2048, 2048], P(('dp', 'ctx'), 'tensor')
- key_grad: float32 [2048, 512], P(('dp', 'ctx'), 'tensor')
- value_grad: float32 [2048, 512], P(('dp', 'ctx'), 'tensor')
- output_grad: float32 [2048, 2048], P('tensor', ('dp', 'ctx'))
- gate_grad: float32 [2048, 8192], P(('dp', 'ctx'), 'tensor')
- up_grad: float32 [2048, 8192], P(('dp', 'ctx'), 'tensor')
- down_grad: float32 [8192, 2048], P('tensor', ('dp', 'ctx'))
- attention_gain_grad: float32 [2048], P('tensor')
- feedforward_gain_grad: float32 [2048], P('tensor')
The draws below stay inside these ranges and needn't reach their ends.
Inputs may be any that keep to these rules, and one draw needn't show every extreme that they name: `lengths`: every sequence has at least 512 tokens, and some sequence has exactly 1024.
All inputs are finite; a program needn't handle non-finite values.
Results may differ from the reference program's by a relative error of at most 0.02.
Values may be sent and summed in bfloat16 or wider, within the bound.
No kernel may reach another device: no remote copies, remote signals or barrier semaphores. Data moves between devices by JAX's collectives and lax.ppermute only.
A program may use at most 320 MiB of HBM per device.

```python
import jax
import jax.numpy as jnp
from jax import lax

D = 2048
HEADS = 32
KVH = 8
HD = 64
FF = 8192
MB = 2
LMAX = 1024
NSEQ = 8
N_DP = 4


def draw_lengths(key, part):
    first, second = jax.random.split(key)
    values = jax.random.randint(first, (NSEQ,), LMAX // 2, LMAX + 1)
    longest = jax.random.randint(second, (), 0, NSEQ)
    return jnp.where(jnp.arange(NSEQ) == longest, LMAX, values).astype(jnp.int32)


def shard_levels(stream_key, shape, shards, least, high):
    loudness = 1.0
    for dim, parts in shards:
        heights = jax.random.uniform(jax.random.fold_in(jax.random.fold_in(stream_key, 6), dim), (parts,), jnp.float32, least / len(shards), high / len(shards))
        loudness = loudness * jnp.repeat(jnp.exp(heights), shape[dim] // parts).reshape((-1,) + (1,) * (len(shape) - 1 - dim))
    return loudness


def gaussian(key, extent, deviation, most, shards=(), kind=jnp.bfloat16):
    entries = deviation * jax.random.normal(key, extent, jnp.float32)
    if shards:
        entries = entries * shard_levels(key, extent, shards, -0.22, 0.18)
    return jnp.clip(entries, -most, most).astype(kind)


def setup_inputs(seed: int = 0) -> dict:
    key_list = jax.random.split(jax.random.key(seed), 14)
    return {
        "inputs": gaussian(key_list[0], (NSEQ, LMAX, D), 1.0, 6.0, ((0, 4), (1, 4), (2, 2))),
        "cotangent": gaussian(key_list[1], (NSEQ, LMAX, D), 1.0, 6.0, ((0, 4), (1, 4), (2, 2))),
        "lengths": draw_lengths(jax.random.fold_in(key_list[13], 71), 0),
        "deal_order": jax.random.permutation(key_list[3], NSEQ).astype(jnp.int32),
        "query_weight": gaussian(key_list[4], (D, HEADS * HD), D ** -0.5, 0.125, ((0, 4), (1, 2))),
        "key_weight": gaussian(key_list[5], (D, KVH * HD), D ** -0.5, 0.125, ((0, 4), (1, 2))),
        "value_weight": gaussian(key_list[6], (D, KVH * HD), D ** -0.5, 0.125, ((0, 4), (1, 2))),
        "output_weight": gaussian(key_list[7], (HEADS * HD, D), (max(HEADS * HD // 256, 4)) ** -0.5, 2.0, ((0, 2), (1, 4))),
        "gate_weight": gaussian(key_list[8], (D, FF), D ** -0.5, 0.125, ((0, 4), (1, 2))),
        "up_weight": gaussian(key_list[9], (D, FF), D ** -0.5, 0.125, ((0, 4), (1, 2))),
        "down_weight": gaussian(key_list[10], (FF, D), FF ** -0.5, 0.0625, ((0, 2), (1, 4))),
        "attention_gain": jnp.clip(1.0 + 0.18 * jax.random.normal(key_list[11], (D,), jnp.float32), 0.1, 1.9),
        "feedforward_gain": jnp.clip(1.0 + 0.18 * jax.random.normal(key_list[12], (D,), jnp.float32), 0.1, 1.9),
    }


EPS = 1e-05
NEGATIVE = -1e+30
HIGH = lax.Precision.HIGHEST

@jax.custom_vjp
def low(v):
    return lax.optimization_barrier(v.astype(jnp.bfloat16)).astype(jnp.float32)

@jax.custom_vjp
def low_back(v):
    return v

def low_keep(v):
    return (low(v), None)

def low_pass(kept, grad):
    return (grad,)

def back_keep(v):
    return (v, None)

def back_low(kept, grad):
    return (low(grad),)
low.defvjp(low_keep, low_pass)
low_back.defvjp(back_keep, back_low)

def inverse_frequency(head_size):
    exponent = jnp.arange(0, head_size, 2, dtype=jnp.int32).astype(jnp.float32) / head_size
    plain = 1.0 / jnp.power(jnp.float32(500000.0), exponent)
    factor = 32.0
    old_context = 8192.0
    wavelength = 2.0 * jnp.pi / plain
    smooth = (old_context / wavelength - 1.0) / (4.0 - 1.0)
    scaled = jnp.where(wavelength > old_context, plain / factor, plain)
    middle = (wavelength <= old_context) & (wavelength >= old_context / 4.0)
    scaled = jnp.where(middle, (1.0 - smooth) * plain / factor + smooth * plain, scaled)
    return scaled.astype(jnp.float32)

def rotate(values, cosine, sine):
    half = values.shape[-1] // 2
    first = values[..., :half]
    second = values[..., half:]
    return jnp.concatenate([first * cosine - second * sine, second * cosine + first * sine], axis=-1)

def rms_norm(values, gain):
    mean_square = lax.optimization_barrier(jnp.mean(values * values, axis=-1, keepdims=True))
    return values * lax.rsqrt(mean_square + EPS) * gain

def attention(query, key, value, length):
    span = query.shape[0]
    block = min(512, span)
    key_pos = jnp.arange(span, dtype=jnp.int32)
    scale = query.shape[-1] ** (-0.5)

    def one_block(index):
        start = (index * block).astype(jnp.int32)
        part = lax.dynamic_slice_in_dim(query, start, block, 0)
        raw = low_back(jnp.einsum('tkgd,pkd->tkgp', part, key, precision=HIGH))
        scores = raw * scale
        query_pos = start + jnp.arange(block, dtype=jnp.int32)
        allowed = ((key_pos[None, :] <= query_pos[:, None]) & (key_pos[None, :] < length))[:, None, None, :]
        masked = jnp.where(allowed, scores, NEGATIVE)
        shifted = masked - lax.optimization_barrier(jnp.max(masked, axis=3, keepdims=True))
        powers = jnp.exp(shifted)
        probs = low(powers / lax.optimization_barrier(jnp.sum(powers, axis=3, keepdims=True)))
        return jnp.einsum('tkgp,pkd->tkgd', probs, value, precision=HIGH)
    blocks = lax.map(jax.checkpoint(one_block), jnp.arange(span // block, dtype=jnp.int32))
    return blocks.reshape(span, -1)

def layer(inputs, length, params):
    query_w, key_w, value_w, output_w, gate_w, up_w, down_w, attention_gain, feedforward_gain = params
    span = inputs.shape[0]
    key_heads = key_w.shape[1] // HD
    ratio = query_w.shape[1] // key_w.shape[1]
    positions = jnp.arange(span, dtype=jnp.int32).astype(jnp.float32)
    angle = positions[:, None] * inverse_frequency(HD)[None, :]
    cosine = jnp.cos(angle)
    sine = jnp.sin(angle)
    normed = low(rms_norm(inputs, attention_gain))
    query = low_back(jnp.dot(normed, query_w, precision=HIGH, preferred_element_type=jnp.float32)).reshape(span, key_heads, ratio, HD)
    key = low_back(jnp.dot(normed, key_w, precision=HIGH, preferred_element_type=jnp.float32)).reshape(span, key_heads, HD)
    value = low(low_back(jnp.dot(normed, value_w, precision=HIGH, preferred_element_type=jnp.float32))).reshape(span, key_heads, HD)
    query = low(rotate(query, cosine[:, None, None, :], sine[:, None, None, :]))
    key = low(rotate(key, cosine[:, None, :], sine[:, None, :]))
    attended = low(low_back(attention(query, key, value, length)))
    hidden = inputs + low_back(jnp.dot(attended, output_w, precision=HIGH, preferred_element_type=jnp.float32))
    normed_two = low(rms_norm(hidden, feedforward_gain))
    gate = low_back(jnp.dot(normed_two, gate_w, precision=HIGH, preferred_element_type=jnp.float32))
    upward = low_back(jnp.dot(normed_two, up_w, precision=HIGH, preferred_element_type=jnp.float32))
    active = low(gate * jax.nn.sigmoid(gate) * upward)
    return hidden + low_back(jnp.dot(active, down_w, precision=HIGH, preferred_element_type=jnp.float32))

def reference(inputs, cotangent, lengths, deal_order, query_weight, key_weight, value_weight, output_weight, gate_weight, up_weight, down_weight, attention_gain, feedforward_gain):
    params = tuple((item.astype(jnp.float32) for item in (query_weight, key_weight, value_weight, output_weight, gate_weight, up_weight, down_weight, attention_gain, feedforward_gain)))
    sequences = lengths.shape[0]
    group_totals = lax.optimization_barrier(jnp.sum(lengths[deal_order].reshape(N_DP, MB), axis=1))
    owner = jnp.zeros((sequences,), jnp.int32).at[deal_order].set(jnp.arange(sequences, dtype=jnp.int32) // MB)
    scale = jnp.sum(lengths).astype(jnp.float32) / N_DP / group_totals[owner].astype(jnp.float32)
    valid = jnp.arange(LMAX, dtype=jnp.int32)[None, :] < lengths[:, None]
    target = cotangent.astype(jnp.float32) * valid[:, :, None] * scale[:, None, None]

    def run_all(values, weights):

        def one(carry, items):
            single, length = items
            return (carry, jax.checkpoint(layer)(single, length, weights))
        unused, outs = lax.scan(one, jnp.float32(0.0), (values, lengths))
        return outs
    outs, pullback = jax.vjp(run_all, inputs.astype(jnp.float32), params)
    input_grad, weight_grads = pullback(target)
    outputs = jnp.where(valid[:, :, None], outs, 0.0).astype(jnp.bfloat16)
    return (outputs, input_grad.astype(jnp.bfloat16), weight_grads[0], weight_grads[1], weight_grads[2], weight_grads[3], weight_grads[4], weight_grads[5], weight_grads[6], weight_grads[7], weight_grads[8])
```

```python
import jax
import jax.numpy as jnp
from jax import lax
from jax.sharding import PartitionSpec as P

HD = 64
EPS = 1e-05
NEGATIVE = -1e30
BF = jnp.bfloat16


def inverse_frequency(head_size):
    exponent = jnp.arange(0, head_size, 2, dtype=jnp.int32).astype(jnp.float32) / head_size
    plain = 1.0 / jnp.power(jnp.float32(500000.0), exponent)
    factor = 32.0
    old_context = 8192.0
    wavelength = 2.0 * jnp.pi / plain
    smooth = (old_context / wavelength - 1.0) / (4.0 - 1.0)
    scaled = jnp.where(wavelength > old_context, plain / factor, plain)
    middle = (wavelength <= old_context) & (wavelength >= old_context / 4.0)
    scaled = jnp.where(middle, (1.0 - smooth) * plain / factor + smooth * plain, scaled)
    return scaled


def rotate(values, cosine, sine):
    half = values.shape[-1] // 2
    first = values[..., :half]
    second = values[..., half:]
    return jnp.concatenate(
        [first * cosine - second * sine, second * cosine + first * sine], axis=-1
    )


def matmul(left, right):
    return jnp.dot(left, right, preferred_element_type=jnp.float32)


class Plan:
    def __init__(self):
        self.place = lax.axis_index("ctx")
        self.side = lax.axis_index("tensor")
        self.group = lax.axis_index("dp")
        self.parts = lax.axis_size("ctx")
        self.sides = lax.axis_size("tensor")
        self.groups = lax.axis_size("dp")
        self.fast = self.parts == 4 and self.sides == 2
        self.core = self.place % 2
        self.masks = (0, 2, 1, 3) if self.fast else tuple(range(self.parts))

    def member(self, block):
        return self.place ^ self.masks[block] if self.fast else block

    def half(self, index):
        return self.side ^ index if self.fast else index

    def ordered(self, block, count):
        return block ^ (self.side * (count // 2)) if self.fast else block


def swap(values, axis, mask):
    size = lax.axis_size(axis)
    return lax.ppermute(values, axis, [(i, i ^ mask) for i in range(size)])


def shift(values, axis, step):
    size = lax.axis_size(axis)
    return lax.ppermute(values, axis, [(i, (i + step) % size) for i in range(size)])


def turn(values, first):
    pairs = []
    for i in range(8):
        along_tensor = (((i >> 1) & 1) == 0) == first
        pairs.append((i, i ^ 1 if along_tensor else i ^ 4))
    return lax.ppermute(values, ("ctx", "tensor"), pairs)


def gather_rows(plan, values):
    if not plan.fast:
        wide = lax.all_gather(values, "tensor", axis=2, tiled=True)
        return lax.all_gather(wide, "ctx", axis=0)
    one = turn(values, True)
    two = turn(values, False)
    far = turn(one, False)
    core_own = swap(values, "ctx", 1)
    core_one = swap(one, "ctx", 1)
    core_two = swap(two, "ctx", 1)
    core_far = swap(far, "ctx", 1)
    zero = plan.core == 0
    rows = [
        jnp.concatenate([values, jnp.where(zero, one, two)], axis=2),
        jnp.concatenate([jnp.where(zero, two, one), far], axis=2),
        jnp.concatenate([core_own, jnp.where(zero, core_two, core_one)], axis=2),
        jnp.concatenate([jnp.where(zero, core_one, core_two), core_far], axis=2),
    ]
    return jnp.stack(rows)


def scatter_rows(plan, left, right, slots):
    width = right.shape[-1]
    if not plan.fast:
        whole = matmul(left, right).astype(BF).reshape(plan.parts, slots, -1, width)
        narrow = lax.psum_scatter(whole, "tensor", scatter_dimension=3, tiled=True)
        return lax.psum_scatter(narrow, "ctx", scatter_dimension=0, tiled=False).astype(jnp.float32)
    half = left.shape[0] // 2
    away = matmul(left[half:], right).astype(BF).reshape(2, slots, -1, width)
    here = matmul(left[:half], right).astype(BF).reshape(2, slots, -1, width)
    return scatter_blocks(plan, here, away)


def add(left, right):
    return (left.astype(jnp.float32) + right.astype(jnp.float32)).astype(BF)


def scatter_blocks(plan, here, away):
    width = here.shape[-1] // 2
    both = add(here, swap(away, "ctx", 1))
    zero = plan.core == 0
    near = both[0, :, :, :width]
    by_tensor = both[0, :, :, width:]
    by_ctx = both[1, :, :, :width]
    far = both[1, :, :, width:]
    got = turn(jnp.stack([jnp.where(zero, by_ctx, by_tensor), far]), False)
    kept = add(near, got[0])
    sent = add(jnp.where(zero, by_tensor, by_ctx), got[1])
    return kept.astype(jnp.float32) + turn(sent, True).astype(jnp.float32)


def exchange_pieces(plan, piece):
    found = [(plan.place, piece(plan.place))]
    for mask in range(1, plan.parts):
        other = plan.place ^ mask
        found.append((other, swap(piece(other), "ctx", mask)))
    return found


def place_rows(plan, found, total):
    rows, columns = found[0][1].shape
    whole = jnp.zeros((total, columns), found[0][1].dtype)
    for member, piece in found:
        start = plan.ordered(member, plan.parts) * rows
        whole = lax.dynamic_update_slice(whole, piece, (start, 0))
    return whole


def place_columns(plan, found, total):
    rows, columns = found[0][1].shape
    whole = jnp.zeros((rows, total), found[0][1].dtype)
    for member, piece in found:
        start = plan.ordered(member, plan.parts) * columns
        whole = lax.dynamic_update_slice(whole, piece, (0, start))
    return whole


def column_piece(weights, parts, least=1):
    def piece(member):
        taken = []
        for weight in weights:
            share = max(1, least * parts // weight.shape[1])
            size = weight.shape[1] * share // parts
            taken.append(lax.dynamic_slice_in_dim(weight, member // share * size, size, 1))
        return jnp.concatenate(taken, axis=1)

    return piece


def row_piece(weight, parts):
    size = weight.shape[0] // parts

    def piece(member):
        return lax.dynamic_slice_in_dim(weight, member * size, size, 0)

    return piece


def reduce_groups(plan, block):
    count = plan.groups
    size = block(plan.group).shape[0] // 2

    def up_block(step):
        return block((plan.group + step) % count)[:size]

    def down_block(step):
        return block((plan.group - step) % count)[size:]

    up = up_block(count - 1).astype(BF)
    down = down_block(count - 1).astype(BF)
    for step in range(count - 2, -1, -1):
        up = add(shift(up, "dp", 1), up_block(step))
        down = add(shift(down, "dp", -1), down_block(step))
    return jnp.concatenate([up, down], axis=0)


def finish_columns(plan, grad, widths):
    rows = grad.shape[0] // plan.groups

    def block(group):
        return lax.dynamic_slice_in_dim(grad, plan.ordered(group, plan.groups) * rows, rows, 0)

    part = reduce_groups(plan, block)
    found = exchange_pieces(plan, row_piece(part, plan.parts))
    outs = []
    start = 0
    for width, share in widths:
        whole = jnp.zeros((rows // plan.parts, width * plan.parts // share), jnp.float32)
        for member, piece in found:
            part = piece[:, start : start + width].astype(jnp.float32)
            at = member // share * width
            if share > 1:
                part = part + lax.dynamic_slice_in_dim(whole, at, width, 1)
            whole = lax.dynamic_update_slice(whole, part, (0, at))
        outs.append(whole)
        start += width
    return outs


def finish_rows(plan, grad):
    columns = grad.shape[1] // plan.groups
    height = grad.shape[0]

    def block(group):
        return lax.dynamic_slice_in_dim(
            grad, plan.ordered(group, plan.groups) * columns, columns, 1
        )

    part = reduce_groups(plan, block)
    found = exchange_pieces(plan, column_piece([part], plan.parts))
    whole = jnp.zeros((height * plan.parts, columns // plan.parts), jnp.float32)
    for member, piece in found:
        whole = lax.dynamic_update_slice(whole, piece.astype(jnp.float32), (member * height, 0))
    return whole


def feature_total(values):
    total = jnp.sum(values, axis=-1, keepdims=True)
    if lax.axis_size("tensor") == 2:
        return total + swap(total, "tensor", 1)
    return lax.psum(total, "tensor")


def per_device(
    inputs,
    cotangent,
    lengths,
    deal_order,
    query_weight,
    key_weight,
    value_weight,
    output_weight,
    gate_weight,
    up_weight,
    down_weight,
    attention_gain,
    feedforward_gain,
):
    plan = Plan()
    slots, rows, half_width = inputs.shape
    width = half_width * plan.sides
    parts = plan.parts
    groups = plan.groups
    sequences = lengths.shape[0]
    tokens = parts * slots * rows
    ids = jnp.arange(sequences, dtype=jnp.int32)
    own_ids = plan.group * slots + jnp.arange(slots, dtype=jnp.int32)
    slot_lengths = lax.dynamic_slice_in_dim(lengths, plan.group * slots, slots)
    dealt = jnp.sum(jnp.where(deal_order[:, None] == ids[None, :], lengths[None, :], 0), axis=1)
    totals = jnp.sum(dealt.reshape(groups, -1), axis=1)
    found = jnp.where(deal_order[None, :] == own_ids[:, None], ids[None, :], 0)
    owner = jnp.sum(found, axis=1) // (sequences // groups)
    mine = owner[:, None] == jnp.arange(groups, dtype=jnp.int32)[None, :]
    own_totals = jnp.sum(jnp.where(mine, totals[None, :], 0), axis=1)
    scale = jnp.sum(lengths).astype(jnp.float32) / groups / own_totals.astype(jnp.float32)

    starts = jnp.stack([plan.member(j) for j in range(parts)]).astype(jnp.int32) * rows
    positions = starts[:, None] + jnp.arange(rows, dtype=jnp.int32)[None, :]
    own_rows = plan.place * rows + jnp.arange(rows, dtype=jnp.int32)
    valid = positions[:, None, :] < slot_lengths[None, :, None]
    own_valid = own_rows[None, :] < slot_lengths[:, None]
    angle = positions.astype(jnp.float32)[:, :, None] * inverse_frequency(HD)
    cosine = jnp.cos(angle)[:, None]
    sine = jnp.sin(angle)[:, None]

    source = inputs.astype(jnp.float32)
    inverse_one = lax.rsqrt(feature_total(source * source) / width + EPS)
    normed = gather_rows(plan, (source * inverse_one * attention_gain).astype(BF))
    normed = normed.reshape(tokens, width)
    qkv_w = place_rows(
        plan, exchange_pieces(plan, column_piece([query_weight, key_weight, value_weight], parts, HD)), width
    )
    o_w = place_columns(plan, exchange_pieces(plan, row_piece(output_weight, parts)), width)
    pair_w = place_rows(
        plan, exchange_pieces(plan, column_piece([gate_weight, up_weight], parts)), width
    )
    down_w = place_columns(plan, exchange_pieces(plan, row_piece(down_weight, parts)), width)
    target_all = gather_rows(plan, cotangent).astype(jnp.float32)
    target_all = (target_all * valid[..., None] * scale[None, :, None, None]).astype(BF)
    target_all = target_all.reshape(tokens, width)

    wide = query_weight.shape[1] // parts
    share = max(1, HD * parts // key_weight.shape[1])
    narrow = key_weight.shape[1] * share // parts
    heads = wide // HD
    projected = matmul(normed, qkv_w)
    query = rotate(
        projected[:, :wide].reshape(parts, slots, rows, heads, HD),
        cosine[..., None, :],
        sine[..., None, :],
    ).astype(BF)
    key = rotate(
        projected[:, wide : wide + narrow].reshape(parts, slots, rows, HD), cosine, sine
    ).astype(BF)
    value = projected[:, wide + narrow :].reshape(parts, slots, rows, HD).astype(BF)
    limit = jnp.minimum(positions[:, None, :] + 1, slot_lengths[None, :, None])
    limit = limit.transpose(1, 0, 2).reshape(slots, 1, parts * rows, 1)
    allowed = positions.reshape(1, 1, 1, parts * rows) < limit

    def by_slot(values):
        return values.swapaxes(0, 1).reshape(slots, parts * rows, *values.shape[3:])

    def by_block(values):
        return values.reshape(slots, parts, rows, -1).swapaxes(0, 1).reshape(tokens, -1)

    query, key, value = by_slot(query), by_slot(key), by_slot(value)
    scores = jnp.einsum("sphd,sqd->shpq", query, key, preferred_element_type=jnp.float32)
    scores = jnp.where(allowed, scores * HD ** (-0.5), NEGATIVE)
    top = jnp.max(scores, axis=3, keepdims=True)
    powers = jnp.where(allowed, jnp.exp(scores - top), 0.0)
    probs = powers / jnp.sum(powers, axis=3, keepdims=True)
    probs_b = probs.astype(BF)
    attended = jnp.einsum("shpq,sqd->sphd", probs_b, value, preferred_element_type=jnp.float32)
    attended_b = by_block(attended.astype(BF))
    hidden = source + scatter_rows(plan, attended_b, o_w, slots)

    inverse_two = lax.rsqrt(feature_total(hidden * hidden) / width + EPS)
    normed_two = gather_rows(plan, (hidden * inverse_two * feedforward_gain).astype(BF))
    normed_two = normed_two.reshape(tokens, width)
    units = pair_w.shape[1] // 2
    gate = matmul(normed_two, pair_w[:, :units])
    upward = matmul(normed_two, pair_w[:, units:])
    sigmoid = jax.nn.sigmoid(gate)
    active = (gate * sigmoid * upward).astype(BF)
    result = hidden + scatter_rows(plan, active, down_w, slots)
    outputs = jnp.where(own_valid[:, :, None], result, 0.0).astype(BF)

    target = cotangent.astype(jnp.float32) * own_valid[:, :, None] * scale[:, None, None]
    grad_active = matmul(target_all, down_w.T)
    down_sum = matmul(active.T, target_all).astype(BF)
    grad_gate = (grad_active * upward * sigmoid * (1.0 + gate * (1.0 - sigmoid))).astype(BF)
    grad_up = (grad_active * gate * sigmoid).astype(BF)
    grad_pair = jnp.concatenate([grad_gate, grad_up], axis=1)
    pair_sum = matmul(normed_two.T, grad_pair).astype(BF)
    dn = scatter_rows(plan, grad_pair, pair_w.T, slots)
    weighted = dn * feedforward_gain
    total_two = feature_total(weighted * hidden)
    grad_hidden = target + inverse_two * weighted - hidden * inverse_two**3 * total_two / width
    gain_two_sum = jnp.sum(dn * hidden * inverse_two, axis=(0, 1))

    grad_hidden_all = gather_rows(plan, grad_hidden.astype(BF)).reshape(tokens, width)
    grad_attended = matmul(grad_hidden_all, o_w.T).astype(BF)
    output_sum = matmul(attended_b.T, grad_hidden_all).astype(BF)
    grad_attended = by_slot(grad_attended.reshape(parts, slots, rows, heads, HD))
    delta = jnp.sum(grad_attended.astype(jnp.float32) * attended, axis=3).transpose(0, 2, 1)
    grad_probs = jnp.einsum(
        "sphd,sqd->shpq", grad_attended, value, preferred_element_type=jnp.float32
    )
    grad_scores = (probs * (grad_probs - delta[..., None]) * HD ** (-0.5)).astype(BF)
    grad_query = jnp.einsum("shpq,sqd->sphd", grad_scores, key, preferred_element_type=jnp.float32)
    grad_key = jnp.einsum("shpq,sphd->sqd", grad_scores, query, preferred_element_type=jnp.float32)
    grad_value = jnp.einsum(
        "shpq,sphd->sqd", probs_b, grad_attended, preferred_element_type=jnp.float32
    )
    cosine_rows = cosine.reshape(parts * rows, -1)
    sine_rows = sine.reshape(parts * rows, -1)
    back_query = rotate(grad_query, cosine_rows[:, None], -sine_rows[:, None]).astype(BF)
    back_key = rotate(grad_key, cosine_rows, -sine_rows).astype(BF)
    back_value = grad_value.astype(BF)
    back = jnp.concatenate([by_block(back_query), by_block(back_key), by_block(back_value)], axis=1)
    dm = scatter_rows(plan, back, qkv_w.T, slots)
    qkv_sum = matmul(normed.T, back).astype(BF)
    weighted = dm * attention_gain
    total_one = feature_total(weighted * source)
    input_grad = grad_hidden + inverse_one * weighted - source * inverse_one**3 * total_one / width
    gain_one_sum = jnp.sum(dm * source * inverse_one, axis=(0, 1))

    gain_one_out, gain_two_out = lax.psum((gain_one_sum, gain_two_sum), ("dp", "ctx"))
    down_out = finish_rows(plan, down_sum)
    gate_out, up_out = finish_columns(plan, pair_sum, ((units, 1), (units, 1)))
    output_out = finish_rows(plan, output_sum)
    query_out, key_out, value_out = finish_columns(
        plan, qkv_sum, ((wide, 1), (narrow, share), (narrow, share))
    )
    return (
        outputs,
        input_grad.astype(BF),
        query_out,
        key_out,
        value_out,
        output_out,
        gate_out,
        up_out,
        down_out,
        gain_one_out,
        gain_two_out,
    )


def solution(mesh):
    return jax.shard_map(
        per_device,
        mesh=mesh,
        in_specs=(
            P("dp", "ctx", "tensor"),
            P("dp", "ctx", "tensor"),
            P(),
            P(),
            P("ctx", "tensor"),
            P("ctx", "tensor"),
            P("ctx", "tensor"),
            P("tensor", "ctx"),
            P("ctx", "tensor"),
            P("ctx", "tensor"),
            P("tensor", "ctx"),
            P("tensor"),
            P("tensor"),
        ),
        out_specs=(
            P("dp", "ctx", "tensor"),
            P("dp", "ctx", "tensor"),
            P(("dp", "ctx"), "tensor"),
            P(("dp", "ctx"), "tensor"),
            P(("dp", "ctx"), "tensor"),
            P("tensor", ("dp", "ctx")),
            P(("dp", "ctx"), "tensor"),
            P(("dp", "ctx"), "tensor"),
            P("tensor", ("dp", "ctx")),
            P("tensor"),
            P("tensor"),
        ),
        check_vma=False,
    )
```

```python
import functools

import jax
import jax.numpy as jnp
from jax import lax
from jax.experimental import pallas as pl
from jax.experimental.pallas import tpu as pltpu
from jax.sharding import PartitionSpec as P

HD = 64
EPS = 1e-05
NEGATIVE = -1e30
BF = jnp.bfloat16


def inverse_frequency(head_size):
    exponent = jnp.arange(0, head_size, 2, dtype=jnp.int32).astype(jnp.float32) / head_size
    plain = 1.0 / jnp.power(jnp.float32(500000.0), exponent)
    factor = 32.0
    old_context = 8192.0
    wavelength = 2.0 * jnp.pi / plain
    smooth = (old_context / wavelength - 1.0) / (4.0 - 1.0)
    scaled = jnp.where(wavelength > old_context, plain / factor, plain)
    middle = (wavelength <= old_context) & (wavelength >= old_context / 4.0)
    scaled = jnp.where(middle, (1.0 - smooth) * plain / factor + smooth * plain, scaled)
    return scaled


def rotation_tables(span):
    positions = jnp.arange(span, dtype=jnp.int32).astype(jnp.float32)
    angle = positions[:, None] * inverse_frequency(HD)[None, :]
    cosine = jnp.cos(angle)
    sine = jnp.sin(angle)
    one = jnp.ones((span, HD), jnp.float32)
    turning = jnp.concatenate([cosine, cosine], axis=1)
    crossing = jnp.concatenate([-sine, sine], axis=1)
    return jnp.stack(
        [
            jnp.concatenate([turning, turning], axis=1),
            jnp.concatenate([crossing, crossing], axis=1),
            jnp.concatenate([turning, one], axis=1),
            jnp.concatenate([crossing, 0.0 * one], axis=1),
        ]
    )


def rotate_lanes(values, tables, rows, sign):
    chunks = values.shape[1] // 128
    lanes = lax.broadcasted_iota(jnp.int32, (values.shape[0], 128), 1)
    first = lanes % HD < HD // 2
    turned = []
    for chunk in range(chunks):
        part = values[:, chunk * 128 : chunk * 128 + 128]
        other = jnp.where(
            first, pltpu.roll(part, 128 - HD // 2, 1), pltpu.roll(part, HD // 2, 1)
        )
        table = 2 if chunk == chunks - 1 else 0
        turned.append(part * tables[table, rows] + sign * other * tables[table + 1, rows])
    return jnp.concatenate(turned, axis=1)


def split_heads(refs, values, rows, heads):
    for head in range(heads):
        refs[0][head, rows] = values[:, head * HD : head * HD + HD]
    if len(refs) > 1:
        refs[1][rows] = values[:, heads * HD : heads * HD + HD]
        refs[2][rows] = values[:, heads * HD + HD :]


def masked_probs(query, keys, limit):
    scores = lax.dot_general(
        query, keys, (((1,), (1,)), ((), ())), preferred_element_type=jnp.float32
    )
    columns = lax.broadcasted_iota(jnp.int32, scores.shape, 1)
    scores = jnp.where(columns < limit, scores * HD ** (-0.5), NEGATIVE)
    powers = jnp.exp(scores - jnp.max(scores, axis=1, keepdims=True))
    return powers * (1.0 / jnp.sum(powers, axis=1, keepdims=True))


def row_limit(start, rows, length):
    positions = start + lax.broadcasted_iota(jnp.int32, (rows, 1), 0)
    return jnp.minimum(positions + 1, length)


def forward_kernel(heads, order, lengths, projected, tables, rotated, attended, qs, ks, vs, outs):
    blocks, _, rows, _ = projected.shape
    length = lengths[pl.program_id(0)]
    for block in range(blocks):
        where = pl.ds(block * rows, rows)
        turned = rotate_lanes(projected[order[block], 0], tables, where, 1.0).astype(BF)
        rotated[order[block], 0] = turned
        split_heads((qs, ks, vs), turned, where, heads)
    for block in range(blocks):
        where = pl.ds(block * rows, rows)
        extent = (block + 1) * rows
        limit = row_limit(block * rows, rows, length)

        def one_head(head, carry):
            probs = masked_probs(qs[head, where], ks[:extent], limit).astype(BF)
            outs[head] = matmul(probs, vs[:extent]).astype(BF)
            return carry

        lax.fori_loop(0, heads, one_head, 0)
        attended[order[block], 0] = jnp.concatenate([outs[h] for h in range(heads)], axis=1)


def backward_kernel(
    heads, order, lengths, rotated, grads, tables, back, qs, ks, vs, gs, dqs, dks, dvs
):
    blocks, _, rows, _ = rotated.shape
    length = lengths[pl.program_id(0)]
    scale = HD ** (-0.5)
    for block in range(blocks):
        where = pl.ds(block * rows, rows)
        split_heads((qs, ks, vs), rotated[order[block], 0], where, heads)
        split_heads((gs,), grads[order[block], 0], where, heads)
    dks[...] = jnp.zeros_like(dks)
    dvs[...] = jnp.zeros_like(dvs)
    for block in range(blocks):
        where = pl.ds(block * rows, rows)
        extent = (block + 1) * rows
        limit = row_limit(block * rows, rows, length)

        def one_head(head, carry):
            query = qs[head, where]
            grad = gs[head, where]
            keys = ks[:extent]
            probs = masked_probs(query, keys, limit)
            grad_probs = lax.dot_general(
                grad, vs[:extent], (((1,), (1,)), ((), ())), preferred_element_type=jnp.float32
            )
            delta = jnp.sum(probs * grad_probs, axis=1, keepdims=True)
            grad_scores = (probs * ((grad_probs - delta) * scale)).astype(BF)
            dqs[head, where] = matmul(grad_scores, keys)
            down = (((0,), (0,)), ((), ()))
            dks[:extent] += lax.dot_general(
                grad_scores, query, down, preferred_element_type=jnp.float32
            )
            dvs[:extent] += lax.dot_general(
                probs.astype(BF), grad, down, preferred_element_type=jnp.float32
            )
            return carry

        lax.fori_loop(0, heads, one_head, 0)
    for block in range(blocks):
        where = pl.ds(block * rows, rows)
        parts = [dqs[h, where] for h in range(heads)] + [dks[where], dvs[where]]
        turned = rotate_lanes(jnp.concatenate(parts, axis=1), tables, where, -1.0)
        back[order[block], 0] = turned.astype(BF)


def slot_spec(shape):
    blocks, _, rows, columns = shape
    return pl.BlockSpec((blocks, 1, rows, columns), lambda slot, *_: (0, slot, 0, 0))


def attention_call(kernel, backward, order, lengths, arrays, tables, outs, scratch, heads):
    blocks, slots, rows, _ = arrays[0].shape
    span = blocks * rows
    work = slots * heads * span * span * HD * (10 if backward else 4) * 5 // 8
    return pl.pallas_call(
        functools.partial(kernel, heads),
        grid_spec=pltpu.PrefetchScalarGridSpec(
            num_scalar_prefetch=2,
            grid=(slots,),
            in_specs=[slot_spec(item.shape) for item in arrays]
            + [pl.BlockSpec(tables.shape, lambda slot, *_: (0, 0, 0))],
            out_specs=[slot_spec(item.shape) for item in outs],
            scratch_shapes=scratch,
        ),
        out_shape=outs,
        compiler_params=pltpu.CompilerParams(vmem_limit_bytes=48 * 2**20),
        cost_estimate=pl.CostEstimate(
            flops=work * 4, bytes_accessed=16 * 2**20, transcendentals=slots * heads * span * span
        ),
    )(order, lengths, *arrays, tables)


def attention_forward(projected, tables, order, lengths):
    blocks, slots, rows, columns = projected.shape
    heads = columns // HD - 2
    span = blocks * rows
    outs = [
        jax.ShapeDtypeStruct(projected.shape, BF),
        jax.ShapeDtypeStruct((blocks, slots, rows, heads * HD), BF),
    ]
    scratch = [
        pltpu.VMEM((heads, span, HD), BF),
        pltpu.VMEM((span, HD), BF),
        pltpu.VMEM((span, HD), BF),
        pltpu.VMEM((heads, rows, HD), BF),
    ]
    return attention_call(
        forward_kernel, False, order, lengths, [projected], tables, outs, scratch, heads
    )


def attention_backward(rotated, grads, tables, order, lengths):
    blocks, slots, rows, columns = rotated.shape
    heads = columns // HD - 2
    span = blocks * rows
    scratch = [
        pltpu.VMEM((heads, span, HD), BF),
        pltpu.VMEM((span, HD), BF),
        pltpu.VMEM((span, HD), BF),
        pltpu.VMEM((heads, span, HD), BF),
        pltpu.VMEM((heads, span, HD), jnp.float32),
        pltpu.VMEM((span, HD), jnp.float32),
        pltpu.VMEM((span, HD), jnp.float32),
    ]
    outs = [jax.ShapeDtypeStruct(rotated.shape, BF)]
    return attention_call(
        backward_kernel, True, order, lengths, [rotated, grads], tables, outs, scratch, heads
    )[0]


def matmul(left, right):
    return jnp.dot(left, right, preferred_element_type=jnp.float32)


class Plan:
    def __init__(self):
        self.place = lax.axis_index("ctx")
        self.side = lax.axis_index("tensor")
        self.group = lax.axis_index("dp")
        self.parts = lax.axis_size("ctx")
        self.sides = lax.axis_size("tensor")
        self.groups = lax.axis_size("dp")
        self.fast = self.parts == 4 and self.sides == 2 and self.groups == 4
        self.core = self.place % 2
        self.masks = (0, 2, 1, 3) if self.fast else tuple(range(self.parts))

    def member(self, block):
        return self.place ^ self.masks[block] if self.fast else block

    def storage(self):
        if not self.fast:
            return jnp.arange(self.parts, dtype=jnp.int32)
        apart = self.place ^ jnp.arange(self.parts, dtype=jnp.int32)
        return (apart % 2) * 2 + apart // 2

    def half(self, index):
        return self.side ^ index if self.fast else index

    def ordered(self, block, count):
        return block ^ (self.side * (count // 2)) if self.fast else block


def after(values, anchor):
    return lax.optimization_barrier((values, anchor))[0]


def swap(values, axis, mask):
    size = lax.axis_size(axis)
    return lax.ppermute(values, axis, [(i, i ^ mask) for i in range(size)])


def shift(values, axis, step):
    size = lax.axis_size(axis)
    return lax.ppermute(values, axis, [(i, (i + step) % size) for i in range(size)])


def turn(values, first):
    pairs = []
    for i in range(8):
        along_tensor = (((i >> 1) & 1) == 0) == first
        pairs.append((i, i ^ 1 if along_tensor else i ^ 4))
    return lax.ppermute(values, ("ctx", "tensor"), pairs)


def gather_rows(plan, values):
    if not plan.fast:
        wide = lax.all_gather(values, "tensor", axis=2, tiled=True)
        return lax.all_gather(wide, "ctx", axis=0)
    one = turn(values, True)
    two = turn(values, False)
    far = turn(one, False)
    core_own = swap(values, "ctx", 1)
    core_one = swap(one, "ctx", 1)
    core_two = swap(two, "ctx", 1)
    core_far = swap(far, "ctx", 1)
    zero = plan.core == 0
    rows = [
        jnp.concatenate([values, jnp.where(zero, one, two)], axis=2),
        jnp.concatenate([jnp.where(zero, two, one), far], axis=2),
        jnp.concatenate([core_own, jnp.where(zero, core_two, core_one)], axis=2),
        jnp.concatenate([jnp.where(zero, core_one, core_two), core_far], axis=2),
    ]
    return jnp.stack(rows)


def scatter_rows(plan, left, right, slots):
    width = right.shape[-1]
    if not plan.fast:
        whole = matmul(left, right).astype(BF).reshape(plan.parts, slots, -1, width)
        narrow = lax.psum_scatter(whole, "tensor", scatter_dimension=3, tiled=True)
        return lax.psum_scatter(narrow, "ctx", scatter_dimension=0, tiled=False).astype(jnp.float32)
    half = left.shape[0] // 2
    away = matmul(left[half:], right).astype(BF).reshape(2, slots, -1, width)
    here = matmul(left[:half], right).astype(BF).reshape(2, slots, -1, width)
    return scatter_blocks(plan, here, away)


def add(left, right):
    return (left.astype(jnp.float32) + right.astype(jnp.float32)).astype(BF)


def scatter_blocks(plan, here, away):
    width = here.shape[-1] // 2
    both = add(here, swap(away, "ctx", 1))
    zero = plan.core == 0
    near = both[0, :, :, :width]
    by_tensor = both[0, :, :, width:]
    by_ctx = both[1, :, :, :width]
    far = both[1, :, :, width:]
    got = turn(jnp.stack([jnp.where(zero, by_ctx, by_tensor), far]), False)
    kept = add(near, got[0])
    sent = add(jnp.where(zero, by_tensor, by_ctx), got[1])
    return kept.astype(jnp.float32) + turn(sent, True).astype(jnp.float32)


def exchange_pieces(plan, piece, shared=False):
    found = [(plan.place, 0, piece(plan.place))]
    if not (shared and plan.fast):
        for mask in range(1, plan.parts):
            other = plan.place ^ mask
            found.append((other, 0, swap(piece(other), "ctx", mask)))
        return found
    found.append((plan.place ^ 1, 0, swap(piece(plan.place ^ 1), "ctx", 1)))
    size = found[0][2].shape[0] // plan.groups
    got = []
    for mask in (2, 3):
        mine = lax.dynamic_slice_in_dim(piece(plan.place ^ mask), plan.group * size, size, 0)
        got.append(swap(mine, "ctx", mask))
    whole = lax.all_gather(jnp.stack(got), "dp")
    for index, mask in enumerate((2, 3)):
        found.append((plan.place ^ mask, 0, whole[:, index].reshape(-1, whole.shape[-1])))
    return found


def place_rows(plan, found, height):
    columns = found[0][2].shape[1]
    whole = jnp.zeros((height * plan.parts, columns), found[0][2].dtype)
    for member, row, piece in found:
        start = plan.ordered(member, plan.parts) * height + row
        whole = lax.dynamic_update_slice(whole, piece, (start, 0))
    return whole


def place_columns(plan, found, height):
    columns = found[0][2].shape[1]
    whole = jnp.zeros((height, columns * plan.parts), found[0][2].dtype)
    for member, row, piece in found:
        start = plan.ordered(member, plan.parts) * columns
        whole = lax.dynamic_update_slice(whole, piece, (row, start))
    return whole


def column_piece(weights, parts, least=1):
    def piece(member):
        taken = []
        for weight in weights:
            share = max(1, least * parts // weight.shape[1])
            size = weight.shape[1] * share // parts
            taken.append(lax.dynamic_slice_in_dim(weight, member // share * size, size, 1))
        return jnp.concatenate(taken, axis=1)

    return piece


def row_piece(weight, parts):
    size = weight.shape[0] // parts

    def piece(member):
        return lax.dynamic_slice_in_dim(weight, member * size, size, 0)

    return piece


def gradient_kernel(side, left, right, out):
    total = lax.dot_general(
        left[...], right[...], (((0,), (0,)), ((), ())), preferred_element_type=jnp.float32
    )
    out[...] = total.astype(out.dtype).reshape(out.shape)


def weight_gradient(plan, left, right, features_first):
    tokens, height = left.shape
    width = right.shape[1]
    groups = plan.groups
    flip = groups // 2 if plan.fast else 0
    tall = height // groups if features_first else height
    broad = width if features_first else width // groups
    step = min(broad, 1024)
    lines = min(tall, 512)

    def at(i, j, side):
        group, line = (i // (tall // lines), i % (tall // lines)) if features_first else (j, i)
        column = j if features_first else 0
        return (group + flip * side[0]) % groups, line, column

    return pl.pallas_call(
        gradient_kernel,
        grid_spec=pltpu.PrefetchScalarGridSpec(
            num_scalar_prefetch=1,
            grid=(height // lines, width // step),
            in_specs=[
                pl.BlockSpec((tokens, lines), lambda i, j, side: (0, i)),
                pl.BlockSpec((tokens, step), lambda i, j, side: (0, j)),
            ],
            out_specs=pl.BlockSpec((1, lines, step), at),
        ),
        out_shape=jax.ShapeDtypeStruct((groups, tall, broad), BF),
        compiler_params=pltpu.CompilerParams(vmem_limit_bytes=48 * 2**20),
        cost_estimate=pl.CostEstimate(
            flops=2 * tokens * height * width,
            bytes_accessed=2 * (tokens * (height + width) + height * width),
            transcendentals=0,
        ),
    )(plan.side[None].astype(jnp.int32), left, right)


def reduce_groups(grad):
    return lax.psum_scatter(grad, "dp", scatter_dimension=0)


def finish_columns(plan, part, widths):
    rows = part.shape[0]
    found = exchange_pieces(plan, row_piece(part, plan.parts))
    outs = []
    start = 0
    for width, share in widths:
        whole = jnp.zeros((rows // plan.parts, width * plan.parts // share), jnp.float32)
        for member, _, piece in found:
            block = piece[:, start : start + width].astype(jnp.float32)
            at = member // share * width
            if share > 1:
                block = block + lax.dynamic_slice_in_dim(whole, at, width, 1)
            whole = lax.dynamic_update_slice(whole, block, (0, at))
        outs.append(whole)
        start += width
    return outs


def finish_rows(plan, part):
    height, columns = part.shape
    found = exchange_pieces(plan, column_piece([part], plan.parts))
    whole = jnp.zeros((height * plan.parts, columns // plan.parts), jnp.float32)
    for member, _, piece in found:
        whole = lax.dynamic_update_slice(whole, piece.astype(jnp.float32), (member * height, 0))
    return whole


def total_over(values, axis):
    mask = 1
    while mask < lax.axis_size(axis):
        values = values + swap(values, axis, mask)
        mask *= 2
    return values


def feature_total(values):
    total = jnp.sum(values, axis=-1, keepdims=True)
    if lax.axis_size("tensor") == 2:
        return total + swap(total, "tensor", 1)
    return lax.psum(total, "tensor")


def per_device(
    inputs,
    cotangent,
    lengths,
    deal_order,
    query_weight,
    key_weight,
    value_weight,
    output_weight,
    gate_weight,
    up_weight,
    down_weight,
    attention_gain,
    feedforward_gain,
):
    plan = Plan()
    slots, rows, half_width = inputs.shape
    width = half_width * plan.sides
    parts = plan.parts
    groups = plan.groups
    sequences = lengths.shape[0]
    tokens = parts * slots * rows
    ids = jnp.arange(sequences, dtype=jnp.int32)
    own_ids = plan.group * slots + jnp.arange(slots, dtype=jnp.int32)
    slot_lengths = lax.dynamic_slice_in_dim(lengths, plan.group * slots, slots)
    dealt = jnp.sum(jnp.where(deal_order[:, None] == ids[None, :], lengths[None, :], 0), axis=1)
    totals = jnp.sum(dealt.reshape(groups, -1), axis=1)
    found = jnp.where(deal_order[None, :] == own_ids[:, None], ids[None, :], 0)
    owner = jnp.sum(found, axis=1) // (sequences // groups)
    mine = owner[:, None] == jnp.arange(groups, dtype=jnp.int32)[None, :]
    own_totals = jnp.sum(jnp.where(mine, totals[None, :], 0), axis=1)
    scale = jnp.sum(lengths).astype(jnp.float32) / groups / own_totals.astype(jnp.float32)

    starts = jnp.stack([plan.member(j) for j in range(parts)]).astype(jnp.int32) * rows
    positions = starts[:, None] + jnp.arange(rows, dtype=jnp.int32)[None, :]
    own_rows = plan.place * rows + jnp.arange(rows, dtype=jnp.int32)
    valid = positions[:, None, :] < slot_lengths[None, :, None]
    own_valid = own_rows[None, :] < slot_lengths[:, None]
    tables = rotation_tables(parts * rows)
    order = plan.storage()

    source = inputs.astype(jnp.float32)
    inverse_one = lax.rsqrt(feature_total(source * source) / width + EPS)
    normed = gather_rows(plan, (source * inverse_one * attention_gain).astype(BF))
    normed = normed.reshape(tokens, width)
    qkv_w = place_rows(
        plan,
        exchange_pieces(plan, column_piece([query_weight, key_weight, value_weight], parts, HD)),
        query_weight.shape[0],
    )
    late = after((output_weight, gate_weight, up_weight, down_weight, cotangent), normed)
    o_w = place_columns(
        plan, exchange_pieces(plan, row_piece(late[0], parts)), output_weight.shape[0] // parts
    )
    pair_w = place_rows(
        plan,
        exchange_pieces(plan, column_piece([late[1], late[2]], parts), True),
        gate_weight.shape[0],
    )
    down_w = place_columns(
        plan, exchange_pieces(plan, row_piece(late[3], parts), True), down_weight.shape[0] // parts
    )
    target_all = gather_rows(plan, late[4]).astype(jnp.float32)
    target_all = (target_all * valid[..., None] * scale[None, :, None, None]).astype(BF)
    target_all = target_all.reshape(tokens, width)

    wide = query_weight.shape[1] // parts
    share = max(1, HD * parts // key_weight.shape[1])
    narrow = key_weight.shape[1] * share // parts
    projected = matmul(normed, qkv_w).reshape(parts, slots, rows, -1)
    rotated, attended = attention_forward(projected, tables, order, slot_lengths)
    attended = attended.reshape(tokens, wide)
    hidden = source + scatter_rows(plan, attended, o_w, slots)

    inverse_two = lax.rsqrt(feature_total(hidden * hidden) / width + EPS)
    normed_two = gather_rows(plan, (hidden * inverse_two * feedforward_gain).astype(BF))
    normed_two = normed_two.reshape(tokens, width)
    units = pair_w.shape[1] // 2
    gate = matmul(normed_two, pair_w[:, :units])
    upward = matmul(normed_two, pair_w[:, units:])
    sigmoid = jax.nn.sigmoid(gate)
    active = (gate * sigmoid * upward).astype(BF)
    target = cotangent.astype(jnp.float32) * own_valid[:, :, None] * scale[:, None, None]
    grad_active = matmul(target_all, down_w.T)
    grad_gate = (grad_active * upward * sigmoid * (1.0 + gate * (1.0 - sigmoid))).astype(BF)
    grad_up = (grad_active * gate * sigmoid).astype(BF)
    grad_pair = jnp.concatenate([grad_gate, grad_up], axis=1)
    dn = scatter_rows(plan, grad_pair, pair_w.T, slots)
    down_part = reduce_groups(weight_gradient(plan, active, target_all, False))
    pair_part = reduce_groups(weight_gradient(plan, normed_two, grad_pair, True))
    weighted = dn * feedforward_gain
    total_two = feature_total(weighted * hidden)
    grad_hidden = target + inverse_two * weighted - hidden * inverse_two**3 * total_two / width
    gain_two_sum = jnp.sum(dn * hidden * inverse_two, axis=(0, 1))

    grad_hidden_all = gather_rows(plan, grad_hidden.astype(BF)).reshape(tokens, width)
    result = hidden + scatter_rows(plan, after(active, dn), down_w, slots)
    outputs = jnp.where(own_valid[:, :, None], result, 0.0).astype(BF)
    grad_attended = matmul(grad_hidden_all, o_w.T).astype(BF)
    output_part = reduce_groups(weight_gradient(plan, attended, grad_hidden_all, False))
    grad_attended = grad_attended.reshape(parts, slots, rows, wide)
    back = attention_backward(rotated, grad_attended, tables, order, slot_lengths)
    back = back.reshape(tokens, -1)
    dm = scatter_rows(plan, back, qkv_w.T, slots)
    qkv_sum = weight_gradient(plan, normed, back, True)
    qkv_part = reduce_groups(qkv_sum)
    flip = plan.side * (width // 2) if plan.fast else 0
    halves = jnp.sum(
        jnp.roll(qkv_sum.reshape(width, -1).astype(jnp.float32), flip, 0)
        * qkv_w.astype(jnp.float32),
        axis=1,
    )
    if plan.fast:
        gain_one_sum = halves[:half_width] + swap(halves[half_width:], "tensor", 1)
    else:
        gain_one_sum = lax.psum_scatter(halves, "tensor", scatter_dimension=0, tiled=True)
    gain_one_sum = gain_one_sum / attention_gain
    weighted = dm * attention_gain
    total_one = feature_total(weighted * source)
    input_grad = grad_hidden + inverse_one * weighted - source * inverse_one**3 * total_one / width

    gains = total_over(total_over(jnp.stack([gain_one_sum, gain_two_sum]), "ctx"), "dp")
    down_out = finish_rows(plan, down_part)
    gate_out, up_out = finish_columns(plan, pair_part, ((units, 1), (units, 1)))
    output_out = finish_rows(plan, output_part)
    query_out, key_out, value_out = finish_columns(
        plan, qkv_part, ((wide, 1), (narrow, share), (narrow, share))
    )
    return (
        outputs,
        input_grad.astype(BF),
        query_out,
        key_out,
        value_out,
        output_out,
        gate_out,
        up_out,
        down_out,
        gains[0],
        gains[1],
    )


def solution(mesh):
    return jax.shard_map(
        per_device,
        mesh=mesh,
        in_specs=(
            P("dp", "ctx", "tensor"),
            P("dp", "ctx", "tensor"),
            P(),
            P(),
            P("ctx", "tensor"),
            P("ctx", "tensor"),
            P("ctx", "tensor"),
            P("tensor", "ctx"),
            P("ctx", "tensor"),
            P("ctx", "tensor"),
            P("tensor", "ctx"),
            P("tensor"),
            P("tensor"),
        ),
        out_specs=(
            P("dp", "ctx", "tensor"),
            P("dp", "ctx", "tensor"),
            P(("dp", "ctx"), "tensor"),
            P(("dp", "ctx"), "tensor"),
            P(("dp", "ctx"), "tensor"),
            P("tensor", ("dp", "ctx")),
            P(("dp", "ctx"), "tensor"),
            P(("dp", "ctx"), "tensor"),
            P("tensor", ("dp", "ctx")),
            P("tensor"),
            P("tensor"),
        ),
        check_vma=False,
    )
```

```python
import functools

import jax
import jax.numpy as jnp
from jax import lax
from jax.experimental import pallas as pl
from jax.experimental.pallas import tpu as pltpu
from jax.sharding import PartitionSpec as P

HD = 64
EPS = 1e-05
NEGATIVE = -1e30
BF = jnp.bfloat16


def inverse_frequency(head_size):
    exponent = jnp.arange(0, head_size, 2, dtype=jnp.int32).astype(jnp.float32) / head_size
    plain = 1.0 / jnp.power(jnp.float32(500000.0), exponent)
    factor = 32.0
    old_context = 8192.0
    wavelength = 2.0 * jnp.pi / plain
    smooth = (old_context / wavelength - 1.0) / (4.0 - 1.0)
    scaled = jnp.where(wavelength > old_context, plain / factor, plain)
    middle = (wavelength <= old_context) & (wavelength >= old_context / 4.0)
    scaled = jnp.where(middle, (1.0 - smooth) * plain / factor + smooth * plain, scaled)
    return scaled


def rotation_tables(span):
    positions = jnp.arange(span, dtype=jnp.int32).astype(jnp.float32)
    angle = positions[:, None] * inverse_frequency(HD)[None, :]
    cosine = jnp.cos(angle)
    sine = jnp.sin(angle)
    one = jnp.ones((span, HD), jnp.float32)
    turning = jnp.concatenate([cosine, cosine], axis=1)
    crossing = jnp.concatenate([-sine, sine], axis=1)
    return jnp.stack(
        [
            jnp.concatenate([turning, turning], axis=1),
            jnp.concatenate([crossing, crossing], axis=1),
            jnp.concatenate([turning, one], axis=1),
            jnp.concatenate([crossing, 0.0 * one], axis=1),
        ]
    )


def rotate_lanes(values, tables, rows, sign):
    chunks = values.shape[1] // 128
    lanes = lax.broadcasted_iota(jnp.int32, (values.shape[0], 128), 1)
    first = lanes % HD < HD // 2
    turned = []
    for chunk in range(chunks):
        part = values[:, chunk * 128 : chunk * 128 + 128]
        other = jnp.where(
            first, pltpu.roll(part, 128 - HD // 2, 1), pltpu.roll(part, HD // 2, 1)
        )
        table = 2 if chunk == chunks - 1 else 0
        turned.append(part * tables[table, rows] + sign * other * tables[table + 1, rows])
    return jnp.concatenate(turned, axis=1)


def take_block(here, away, index):
    half = here.shape[1]
    return jnp.where(index < half, here[0, index % half], away[0, index % half])


def put_block(here, away, index, values):
    half = here.shape[1]

    @pl.when(index < half)
    def _():
        here[0, index % half] = values

    @pl.when(index >= half)
    def _():
        away[0, index % half] = values


def split_heads(ref, values, rows, heads):
    for head in range(heads):
        ref[head, rows] = values[:, head * HD : head * HD + HD]


def masked_scores(query, keys, limit):
    scores = lax.dot_general(
        query, keys, (((1,), (1,)), ((), ())), preferred_element_type=jnp.float32
    )
    columns = lax.broadcasted_iota(jnp.int32, scores.shape, 1)
    return jnp.where(columns < limit, scores, NEGATIVE)


def row_limit(start, rows, length):
    positions = start + lax.broadcasted_iota(jnp.int32, (rows, 1), 0)
    return jnp.minimum(positions + 1, length)


def forward_kernel(
    heads,
    order,
    lengths,
    projected_here,
    projected_away,
    tables,
    rotated_here,
    rotated_away,
    attended_here,
    attended_away,
    stats,
    qs,
    ks,
    vs,
):
    _, half, rows, _ = projected_here.shape
    blocks = 2 * half
    wide = heads * HD
    length = lengths[pl.program_id(0)]
    lanes = lax.broadcasted_iota(jnp.int32, (rows, 128), 1)
    for block in range(blocks):
        where = pl.ds(block * rows, rows)
        values = take_block(projected_here, projected_away, order[block])
        turned = rotate_lanes(values, tables, where, 1.0).astype(BF)
        put_block(rotated_here, rotated_away, order[block], turned)
        split_heads(qs, turned[:, :wide] * BF(HD ** (-0.5)), where, heads)
        ks[where] = turned[:, wide : wide + HD]
        vs[where] = turned[:, wide + HD :]
    for block in range(blocks):
        where = pl.ds(block * rows, rows)
        extent = (block + 1) * rows
        limit = row_limit(block * rows, rows, length)
        outs = []
        logs = jnp.zeros((rows, 128), jnp.float32)
        for head in range(heads):
            scores = masked_scores(qs[head, where], ks[:extent], limit)
            top = jnp.max(scores, axis=1, keepdims=True)
            powers = jnp.exp(scores - top)
            total = jnp.sum(powers, axis=1, keepdims=True)
            outs.append((matmul(powers.astype(BF), vs[:extent]) * (1.0 / total)).astype(BF))
            logs = jnp.where(lanes == head, top + jnp.log(total), logs)
        stats[0, where] = logs
        put_block(attended_here, attended_away, order[block], jnp.concatenate(outs, axis=1))


def backward_kernel(
    heads,
    order,
    lengths,
    rotated_here,
    rotated_away,
    grads_here,
    grads_away,
    tables,
    stats,
    back_here,
    back_away,
    qs,
    ks,
    vs,
    gs,
    dqs,
    dks,
    dvs,
):
    _, half, rows, _ = rotated_here.shape
    blocks = 2 * half
    wide = heads * HD
    length = lengths[pl.program_id(0)]
    scale = HD ** (-0.5)
    down = (((0,), (0,)), ((), ()))
    for block in range(blocks):
        where = pl.ds(block * rows, rows)
        turned = take_block(rotated_here, rotated_away, order[block])
        split_heads(qs, turned[:, :wide] * BF(scale), where, heads)
        ks[where] = turned[:, wide : wide + HD]
        vs[where] = turned[:, wide + HD :]
        split_heads(gs, take_block(grads_here, grads_away, order[block]), where, heads)
    dks[...] = jnp.zeros_like(dks)
    dvs[...] = jnp.zeros_like(dvs)
    for block in range(blocks):
        where = pl.ds(block * rows, rows)
        extent = (block + 1) * rows
        limit = row_limit(block * rows, rows, length)
        for head in range(heads):
            query = qs[head, where]
            grad = gs[head, where]
            keys = ks[:extent]
            scores = masked_scores(query, keys, limit)
            probs = jnp.exp(scores - stats[0, where][:, head : head + 1])
            grad_probs = lax.dot_general(
                grad, vs[:extent], (((1,), (1,)), ((), ())), preferred_element_type=jnp.float32
            )
            delta = jnp.sum(probs * grad_probs, axis=1, keepdims=True)
            grad_scores = (probs * (grad_probs - delta)).astype(BF)
            dqs[head, where] = matmul(grad_scores, keys) * scale
            dks[:extent] += lax.dot_general(
                grad_scores, query, down, preferred_element_type=jnp.float32
            )
            dvs[:extent] += lax.dot_general(
                probs.astype(BF), grad, down, preferred_element_type=jnp.float32
            )
    for block in range(blocks):
        where = pl.ds(block * rows, rows)
        parts = [dqs[h, where] for h in range(heads)] + [dks[where], dvs[where]]
        turned = rotate_lanes(jnp.concatenate(parts, axis=1), tables, where, -1.0)
        put_block(back_here, back_away, order[block], turned.astype(BF))


def slot_spec(shape):
    rest = tuple(shape[1:])
    return pl.BlockSpec((1, *rest), lambda slot, *_: (slot,) + (0,) * len(rest))


def attention_call(kernel, heads, order, lengths, tables, arrays, extra, outs, scratch, work):
    slots, half, rows, _ = arrays[0].shape
    span = 2 * half * rows
    return pl.pallas_call(
        functools.partial(kernel, heads),
        grid_spec=pltpu.PrefetchScalarGridSpec(
            num_scalar_prefetch=2,
            grid=(slots,),
            in_specs=[slot_spec(item.shape) for item in arrays]
            + [pl.BlockSpec(tables.shape, lambda slot, *_: (0, 0, 0))]
            + [slot_spec(item.shape) for item in extra],
            out_specs=[slot_spec(item.shape) for item in outs],
            scratch_shapes=scratch,
        ),
        out_shape=outs,
        compiler_params=pltpu.CompilerParams(vmem_limit_bytes=48 * 2**20),
        cost_estimate=pl.CostEstimate(
            flops=work * slots * heads * span * span * HD * 5 // 2,
            bytes_accessed=16 * 2**20,
            transcendentals=slots * heads * span * span,
        ),
    )(order, lengths, *arrays, tables, *extra)


def attention_forward(projected, tables, order, lengths):
    slots, half, rows, columns = projected[0].shape
    heads = columns // HD - 2
    span = 2 * half * rows
    rotated = jax.ShapeDtypeStruct(projected[0].shape, BF)
    attended = jax.ShapeDtypeStruct((slots, half, rows, heads * HD), BF)
    stats = jax.ShapeDtypeStruct((slots, span, 128), jnp.float32)
    scratch = [
        pltpu.VMEM((heads, span, HD), BF),
        pltpu.VMEM((span, HD), BF),
        pltpu.VMEM((span, HD), BF),
    ]
    outs = [rotated, rotated, attended, attended, stats]
    found = attention_call(
        forward_kernel, heads, order, lengths, tables, projected, [], outs, scratch, 4
    )
    return tuple(found[:2]), tuple(found[2:4]), found[4]


def attention_backward(rotated, grads, stats, tables, order, lengths):
    slots, half, rows, columns = rotated[0].shape
    heads = columns // HD - 2
    span = 2 * half * rows
    scratch = [
        pltpu.VMEM((heads, span, HD), BF),
        pltpu.VMEM((span, HD), BF),
        pltpu.VMEM((span, HD), BF),
        pltpu.VMEM((heads, span, HD), BF),
        pltpu.VMEM((heads, span, HD), jnp.float32),
        pltpu.VMEM((span, HD), jnp.float32),
        pltpu.VMEM((span, HD), jnp.float32),
    ]
    outs = [jax.ShapeDtypeStruct(rotated[0].shape, BF)] * 2
    arrays = [*rotated, *grads]
    return attention_call(
        backward_kernel, heads, order, lengths, tables, arrays, [stats], outs, scratch, 10
    )


def matmul(left, right):
    return jnp.dot(left, right, preferred_element_type=jnp.float32)


class Plan:
    def __init__(self, slots):
        self.place = lax.axis_index("ctx")
        self.side = lax.axis_index("tensor")
        self.group = lax.axis_index("dp")
        self.parts = lax.axis_size("ctx")
        self.sides = lax.axis_size("tensor")
        self.groups = lax.axis_size("dp")
        self.fast = self.parts == 4 and self.sides == 2 and self.groups == 4 and slots == 2

    def storage(self):
        members = jnp.arange(self.parts, dtype=jnp.int32)
        if not self.fast:
            return members
        apart = self.place ^ members
        return (apart % 2) * 2 + apart // 2

    def members(self, away):
        half = self.parts // 2
        if not self.fast:
            return jnp.arange(half, dtype=jnp.int32) + away * half
        return self.place ^ (2 * jnp.arange(half, dtype=jnp.int32) + away)

    def ordered(self, block, count):
        return block ^ (self.side * (count // 2)) if self.fast else block


def after(values, anchor):
    return lax.optimization_barrier((values, anchor))[0]


def swap(values, axis, mask):
    size = lax.axis_size(axis)
    return lax.ppermute(values, axis, [(i, i ^ mask) for i in range(size)])


def gather_open(plan, values):
    if not plan.fast:
        wide = lax.all_gather(values, "tensor", axis=2, tiled=True)
        return (lax.all_gather(wide, "ctx", axis=0),)
    zero, one = values[0], values[1]
    zero_side = swap(zero, "tensor", 1)
    one_ctx = swap(one, "ctx", 2)
    zero_ctx = swap(zero, "ctx", 2)
    one_side = swap(one, "tensor", 1)
    zero_far = swap(zero_side, "ctx", 2)
    one_far = swap(one_ctx, "tensor", 1)
    return zero, zero_side, zero_ctx, zero_far, one, one_side, one_ctx, one_far


def gather_close(plan, opened, finish=None):
    if finish is None:
        finish = [lambda half: half] * 2
    if not plan.fast:
        half = plan.parts // 2
        whole = opened[0].swapaxes(0, 1)
        return finish[0](whole[:, :half]), finish[1](whole[:, half:])
    opened = lax.optimization_barrier(opened)
    zero, zero_side, zero_ctx, zero_far, one, one_side, one_ctx, one_far = opened
    rows = [
        jnp.concatenate(pair, axis=1)
        for pair in ((zero, zero_side), (zero_ctx, zero_far), (one, one_side), (one_ctx, one_far))
    ]
    here = finish[0](jnp.stack(rows).reshape(2, 2, *rows[0].shape))
    return here, swap(here, "ctx", 1)


def flat(halves):
    return tuple(half.reshape(-1, half.shape[-1]) for half in halves)


def gather_rows(plan, values):
    return flat(gather_close(plan, gather_open(plan, values)))


def wide_sum(*terms):
    return sum(term.astype(jnp.float32) for term in terms)


def scatter_open(plan, lefts, right, slots):
    away = matmul(lefts[1], right).astype(BF)
    here = matmul(lefts[0], right).astype(BF)
    return scatter_halves(plan, here, away, slots)


def scatter_halves(plan, here, away, slots):
    width = here.shape[-1]
    half = plan.parts // 2
    here = here.reshape(slots, half, -1, width)
    away = away.reshape(slots, half, -1, width)
    if not plan.fast:
        return (jnp.concatenate([here, away], axis=1),)
    got = swap(away, "ctx", 1)
    own = width // 2
    zero_sent = wide_sum(here[0, 1], got[0, 1]).astype(BF)
    one_sent = wide_sum(here[1, :, :, own:], got[1, :, :, own:]).astype(BF)
    return here, got, zero_sent, one_sent


def scatter_turn(plan, opened):
    if not plan.fast:
        return opened
    here, got, zero_sent, one_sent = opened
    return here, got, swap(zero_sent, "ctx", 2), swap(one_sent, "tensor", 1)


def scatter_end(plan, turned):
    if not plan.fast:
        whole = turned[0].swapaxes(0, 1)
        narrow = lax.psum_scatter(whole, "tensor", scatter_dimension=3, tiled=True)
        return lax.psum_scatter(narrow, "ctx", scatter_dimension=0, tiled=False).astype(jnp.float32)
    here, got, zero, one = turned
    own = here.shape[-1] // 2
    zero_sent = wide_sum(here[0, 0, :, own:], got[0, 0, :, own:], zero[:, own:]).astype(BF)
    one_sent = wide_sum(here[1, 1, :, :own], got[1, 1, :, :own], one[1]).astype(BF)
    zero_sent, one_sent = lax.optimization_barrier((zero_sent, one_sent))
    zero_last, one_last = lax.optimization_barrier(
        (swap(zero_sent, "tensor", 1), swap(one_sent, "ctx", 2))
    )
    zero_total = wide_sum(here[0, 0, :, :own], got[0, 0, :, :own], zero[:, :own], zero_last)
    one_total = wide_sum(here[1, 0, :, :own], got[1, 0, :, :own], one[0], one_last)
    return jnp.stack([zero_total, one_total])


def scatter_close(plan, opened, beside=None):
    turned = scatter_turn(plan, opened)
    if beside is not None:
        turned = after(turned, beside)
    return scatter_end(plan, turned)


def exchange_pieces(plan, piece):
    found = [piece(plan.place)]
    for mask in range(1, plan.parts):
        found.append(swap(piece(plan.place ^ mask), "ctx", mask))
    return found


def shared_pieces(plan, columns, rows):
    if not plan.fast:
        return exchange_pieces(plan, columns), exchange_pieces(plan, rows)
    count = plan.groups
    narrow = rows(plan.place).shape[1]

    def quarter(piece):
        size = piece.shape[0] // count
        return lax.dynamic_slice_in_dim(piece, plan.group * size, size, 0)

    got = []
    for mask in (2, 3):
        wide = quarter(columns(plan.place ^ mask))
        strips = [wide[:, i : i + narrow] for i in range(0, wide.shape[1], narrow)]
        strips.append(quarter(rows(plan.place ^ mask)))
        got.append(swap(jnp.concatenate(strips), "ctx", mask))
    return jnp.stack(got)


def core_pieces(plan, piece):
    return [piece(plan.place), swap(piece(plan.place ^ 1), "ctx", 1)]


def split_shared(plan, whole, columns, rows):
    if not plan.fast:
        return whole
    whole = lax.all_gather(whole, "dp")
    count = plan.groups
    high = columns[0].shape[0] // count
    strips = columns[0].shape[1] // rows[0].shape[1]
    for index in range(2):
        part = whole[:, index]
        wide = [part[:, i * high : (i + 1) * high].reshape(high * count, -1) for i in range(strips)]
        columns = columns + [jnp.concatenate(wide, axis=1)]
        rows = rows + [part[:, strips * high :].reshape(rows[0].shape)]
    return columns, rows


def place_rows(plan, found):
    rows, columns = found[0].shape
    whole = jnp.zeros((rows * plan.parts, columns), found[0].dtype)
    for mask, piece in enumerate(found):
        start = plan.ordered(plan.place ^ mask, plan.parts) * rows
        whole = lax.dynamic_update_slice(whole, piece, (start, 0))
    return whole


def place_columns(plan, found):
    rows, columns = found[0].shape
    whole = jnp.zeros((rows, columns * plan.parts), found[0].dtype)
    for mask, piece in enumerate(found):
        start = plan.ordered(plan.place ^ mask, plan.parts) * columns
        whole = lax.dynamic_update_slice(whole, piece, (0, start))
    return whole


def by_member(plan, found):
    bit = 1
    while bit < plan.parts:
        flip = (plan.place & bit) != 0
        found = [jnp.where(flip, found[i ^ bit], found[i]) for i in range(plan.parts)]
        bit *= 2
    return found


def column_piece(weights, parts, least=1):
    def piece(member):
        taken = []
        for weight in weights:
            share = max(1, least * parts // weight.shape[1])
            size = weight.shape[1] * share // parts
            taken.append(lax.dynamic_slice_in_dim(weight, member // share * size, size, 1))
        return jnp.concatenate(taken, axis=1)

    return piece


def row_piece(weight, parts):
    size = weight.shape[0] // parts

    def piece(member):
        return lax.dynamic_slice_in_dim(weight, member * size, size, 0)

    return piece


def forward_units_kernel(normed, weights, active, slope_gate, slope_up):
    units = weights.shape[1] // 2
    gate = matmul(normed[...], weights[:, :units])
    upward = matmul(normed[...], weights[:, units:])
    sigmoid = jax.nn.sigmoid(gate)
    swish = gate * sigmoid
    active[...] = (swish * upward).astype(BF)
    slope_gate[...] = (upward * sigmoid * (1.0 + gate * (1.0 - sigmoid))).astype(BF)
    slope_up[...] = swish.astype(BF)


def backward_units_kernel(target, slope_gate, slope_up, down, weights, grads, back):
    units = down.shape[0]
    across = (((1,), (1,)), ((), ()))
    grad = lax.dot_general(target[...], down[...], across, preferred_element_type=jnp.float32)
    grads[:, :units] = (grad * slope_gate[...]).astype(BF)
    grads[:, units:] = (grad * slope_up[...]).astype(BF)
    total = lax.dot_general(grads[...], weights[...], across, preferred_element_type=jnp.float32)
    back[...] = total.astype(BF)


def row_blocks(kernel, blocked, whole, widths):
    lines = blocked[0].shape[0]
    rows = min(512, lines)
    flops = sum(2 * lines * item.shape[0] * item.shape[1] for item in whole)
    moved = sum(2 * lines * item.shape[1] for item in blocked) + sum(2 * lines * w for w in widths)
    return pl.pallas_call(
        kernel,
        grid=(lines // rows,),
        in_specs=[pl.BlockSpec((rows, item.shape[1]), lambda i: (i, 0)) for item in blocked]
        + [pl.BlockSpec(item.shape, lambda i: (0, 0)) for item in whole],
        out_specs=[pl.BlockSpec((rows, width), lambda i: (i, 0)) for width in widths],
        out_shape=[jax.ShapeDtypeStruct((lines, width), BF) for width in widths],
        compiler_params=pltpu.CompilerParams(vmem_limit_bytes=56 * 2**20),
        cost_estimate=pl.CostEstimate(
            flops=flops,
            bytes_accessed=moved + sum(2 * item.size for item in whole),
            transcendentals=0,
        ),
    )(*blocked, *whole)


def forward_units(normed, weights):
    return row_blocks(forward_units_kernel, [normed], [weights], [weights.shape[1] // 2] * 3)


def backward_units(target, slopes, down, weights):
    return row_blocks(
        backward_units_kernel,
        [target, *slopes],
        [down, weights],
        [weights.shape[1], weights.shape[0]],
    )


def gradient_kernel(side, left_here, left_away, right_here, right_away, out):
    total = None
    for left, right in ((left_here, right_here), (left_away, right_away)):
        term = lax.dot_general(
            left[...], right[...], (((0,), (0,)), ((), ())), preferred_element_type=jnp.float32
        )
        total = term if total is None else total + term
    out[...] = total.astype(out.dtype).reshape(out.shape)


def weight_gradient(plan, lefts, rights, features_first, part=0, parts=1):
    tokens, height = lefts[0].shape
    width = rights[0].shape[1] // parts
    groups = plan.groups
    flip = groups // 2 if plan.fast else 0
    tall = height // groups if features_first else height
    broad = width if features_first else width // groups
    step = min(broad, 1024)
    lines = min(tall, 512)
    skip = part * (width // step)

    def at(i, j, side):
        group, line = (i // (tall // lines), i % (tall // lines)) if features_first else (j, i)
        column = j if features_first else 0
        return (group + flip * side[0]) % groups, line, column

    return pl.pallas_call(
        gradient_kernel,
        grid_spec=pltpu.PrefetchScalarGridSpec(
            num_scalar_prefetch=1,
            grid=(height // lines, width // step),
            in_specs=[pl.BlockSpec((tokens, lines), lambda i, j, side: (0, i))] * 2
            + [pl.BlockSpec((tokens, step), lambda i, j, side: (0, j + skip))] * 2,
            out_specs=pl.BlockSpec((1, lines, step), at),
        ),
        out_shape=jax.ShapeDtypeStruct((groups, tall, broad), BF),
        compiler_params=pltpu.CompilerParams(vmem_limit_bytes=48 * 2**20),
        cost_estimate=pl.CostEstimate(
            flops=4 * tokens * height * width,
            bytes_accessed=2 * (2 * tokens * (height + width) + height * width),
            transcendentals=0,
        ),
    )(plan.side[None].astype(jnp.int32), *lefts, *rights)


def reduce_groups(grad):
    return lax.psum_scatter(grad, "dp", scatter_dimension=0)


def finish_columns(plan, found, widths):
    found = by_member(plan, found)
    outs = []
    start = 0
    for width, share in widths:
        blocks = [piece[:, start : start + width].astype(jnp.float32) for piece in found]
        blocks = [sum(blocks[i : i + share]) for i in range(0, plan.parts, share)]
        outs.append(jnp.concatenate(blocks, axis=1))
        start += width
    return outs


def finish_rows(plan, found):
    return jnp.concatenate(by_member(plan, found), axis=0).astype(jnp.float32)


def send_rows(plan, part):
    return exchange_pieces(plan, row_piece(part, plan.parts))


def send_columns(plan, part):
    return exchange_pieces(plan, column_piece([part], plan.parts))


def total_over(values, axis):
    others = [swap(values, axis, mask) for mask in range(1, lax.axis_size(axis))]
    return sum(lax.optimization_barrier(others), values)


def feature_total(values):
    total = jnp.sum(values, axis=-1, keepdims=True)
    if lax.axis_size("tensor") == 2:
        return total + swap(total, "tensor", 1)
    return lax.psum(total, "tensor")


def per_device(
    inputs,
    cotangent,
    lengths,
    deal_order,
    query_weight,
    key_weight,
    value_weight,
    output_weight,
    gate_weight,
    up_weight,
    down_weight,
    attention_gain,
    feedforward_gain,
):
    slots, rows, half_width = inputs.shape
    plan = Plan(slots)
    width = half_width * plan.sides
    parts = plan.parts
    groups = plan.groups
    sequences = lengths.shape[0]
    ids = jnp.arange(sequences, dtype=jnp.int32)
    own_ids = plan.group * slots + jnp.arange(slots, dtype=jnp.int32)
    slot_lengths = lax.dynamic_slice_in_dim(lengths, plan.group * slots, slots)
    dealt = jnp.sum(jnp.where(deal_order[:, None] == ids[None, :], lengths[None, :], 0), axis=1)
    totals = jnp.sum(dealt.reshape(groups, -1), axis=1)
    found = jnp.where(deal_order[None, :] == own_ids[:, None], ids[None, :], 0)
    owner = jnp.sum(found, axis=1) // (sequences // groups)
    mine = owner[:, None] == jnp.arange(groups, dtype=jnp.int32)[None, :]
    own_totals = jnp.sum(jnp.where(mine, totals[None, :], 0), axis=1)
    scale = jnp.sum(lengths).astype(jnp.float32) / groups / own_totals.astype(jnp.float32)

    own_rows = plan.place * rows + jnp.arange(rows, dtype=jnp.int32)
    own_valid = own_rows[None, :] < slot_lengths[:, None]
    tables = rotation_tables(parts * rows)
    order = plan.storage()

    def scaled(away):
        starts = plan.members(away) * rows
        positions = starts[:, None] + jnp.arange(rows, dtype=jnp.int32)[None, :]
        valid = positions[None] < slot_lengths[:, None, None]
        factor = jnp.where(valid, scale[:, None, None], 0.0)
        return lambda half: (half.astype(jnp.float32) * factor[..., None]).astype(BF)

    source = inputs.astype(jnp.float32)
    inverse_one = lax.rsqrt(feature_total(source * source) / width + EPS)
    columns = column_piece([gate_weight, up_weight], parts)
    rows_piece = row_piece(down_weight, parts)
    shared = shared_pieces(plan, columns, rows_piece)
    opened = gather_open(plan, (source * inverse_one * attention_gain).astype(BF))
    qkv_w = place_rows(
        plan,
        exchange_pieces(plan, column_piece([query_weight, key_weight, value_weight], parts, HD)),
    )
    opened, shared = after((opened, shared), (tables, qkv_w))
    normed = gather_close(plan, opened)
    late = after((output_weight, gate_weight, up_weight, down_weight), normed[0])
    o_found = exchange_pieces(plan, row_piece(late[0], parts))
    normed = flat(normed)

    wide = query_weight.shape[1] // parts
    share = max(1, HD * parts // key_weight.shape[1])
    narrow = key_weight.shape[1] * share // parts
    half_shape = (slots, parts // 2, rows, -1)
    projected = [matmul(item, qkv_w).reshape(half_shape) for item in normed]
    rotated, attended, stats = attention_forward(projected, tables, order, slot_lengths)
    attended = flat(attended)
    attended, o_found = after((attended, o_found), rotated)
    o_w = place_columns(plan, o_found)
    opened = scatter_open(plan, attended, o_w, slots)
    hidden = source + scatter_close(plan, opened)
    if plan.fast:
        pair_core = core_pieces(plan, column_piece([late[1], late[2]], parts))
        down_core = core_pieces(plan, row_piece(late[3], parts))
    else:
        pair_core = down_core = None

    inverse_two = lax.rsqrt(feature_total(hidden * hidden) / width + EPS)
    opened = gather_open(plan, (hidden * inverse_two * feedforward_gain).astype(BF))
    pair_found, down_found = split_shared(plan, shared, pair_core, down_core)
    pair_w = place_rows(plan, pair_found)
    normed_two = flat(gather_close(plan, after(opened, pair_w)))
    target_open = gather_open(plan, after(cotangent, normed_two[0]))
    units = pair_w.shape[1] // 2
    active_here, *slopes_here = forward_units(normed_two[0], pair_w)
    normed_two = (normed_two[0], after(normed_two[1], active_here))
    active_away, *slopes_away = forward_units(normed_two[1], pair_w)
    active = (active_here, active_away)
    active, target_open = after((active, target_open), active_away)
    down_w = place_columns(plan, down_found)
    target_all = flat(gather_close(plan, target_open, [scaled(0), scaled(1)]))
    down_sum = weight_gradient(plan, active, target_all, False)
    down_part = reduce_groups(down_sum)

    target = cotangent.astype(jnp.float32) * own_valid[:, :, None] * scale[:, None, None]
    target_away = after(target_all[1], down_sum)
    grads_away, away = backward_units(target_away, slopes_away, down_w, pair_w)
    target_here = after(target_all[0], away)
    grads_here, here = backward_units(target_here, slopes_here, down_w, pair_w)
    grad_pair = (grads_here, grads_away)
    opened = scatter_halves(plan, here, away, slots)
    grad_late = after(grad_pair, opened[-1])
    gate_sum = weight_gradient(plan, normed_two, grad_late, True, 0, 2)
    up_sum = weight_gradient(plan, normed_two, grad_late, True, 1, 2)
    gate_part = reduce_groups(gate_sum)
    up_part = reduce_groups(up_sum)
    dn = scatter_close(plan, opened, (gate_sum, up_sum, down_part))
    weighted = dn * feedforward_gain
    total_two = feature_total(weighted * hidden)
    grad_hidden = target + inverse_two * weighted - hidden * inverse_two**3 * total_two / width
    gain_two_sum = jnp.sum(dn * hidden * inverse_two, axis=(0, 1))

    result_open = scatter_open(plan, after(active, grad_hidden), down_w, slots)
    opened = after(gather_open(plan, grad_hidden.astype(BF)), (result_open, gate_part))
    grad_hidden_all = flat(gather_close(plan, opened))
    result_open, down_part, gate_part = after((result_open, down_part, gate_part), grad_hidden_all)
    result_turned = scatter_turn(plan, result_open)
    down_sent = send_columns(plan, down_part)
    gate_sent = send_rows(plan, gate_part)
    grad_attended = [matmul(item, o_w.T).astype(BF) for item in grad_hidden_all]
    output_sum = weight_gradient(plan, attended, grad_hidden_all, False)
    grad_attended = after(grad_attended, output_sum)
    grad_attended = [item.reshape(half_shape) for item in grad_attended]
    back = attention_backward(rotated, grad_attended, stats, tables, order, slot_lengths)
    sent = (result_turned, down_sent, gate_sent, output_sum)
    back, sent = after((flat(back), sent), back)
    result_turned, down_sent, gate_sent, output_sum = sent
    output_part = reduce_groups(output_sum)
    opened = scatter_open(plan, back, qkv_w.T, slots)
    qkv_sum = weight_gradient(plan, normed, after(back, opened[-1]), True)
    result = hidden + scatter_end(plan, result_turned)
    outputs = jnp.where(own_valid[:, :, None], result, 0.0).astype(BF)
    qkv_part = reduce_groups(qkv_sum)
    dm = scatter_close(plan, opened, (qkv_sum, up_part, outputs))
    up_part = after(up_part, dm)
    up_sent = send_rows(plan, up_part)
    flip = plan.side * (width // 2) if plan.fast else 0
    halves = jnp.sum(
        jnp.roll(qkv_sum.reshape(width, -1).astype(jnp.float32), flip, 0)
        * qkv_w.astype(jnp.float32),
        axis=1,
    )
    if plan.fast:
        gain_one_sum = halves[:half_width] + after(swap(halves[half_width:], "tensor", 1), dm)
    else:
        gain_one_sum = lax.psum_scatter(halves, "tensor", scatter_dimension=0, tiled=True)
    gain_one_sum = gain_one_sum / attention_gain
    weighted = dm * attention_gain
    total_one = feature_total(weighted * source)
    input_grad = grad_hidden + inverse_one * weighted - source * inverse_one**3 * total_one / width

    gains = total_over(total_over(jnp.stack([gain_one_sum, gain_two_sum]), "ctx"), "dp")
    output_part, qkv_part = after((output_part, qkv_part), gains)
    output_sent = send_columns(plan, output_part)
    qkv_sent = send_rows(plan, qkv_part)
    down_out = finish_rows(plan, down_sent)
    (gate_out,) = finish_columns(plan, gate_sent, ((units, 1),))
    (up_out,) = finish_columns(plan, up_sent, ((units, 1),))
    output_out = finish_rows(plan, output_sent)
    query_out, key_out, value_out = finish_columns(
        plan, qkv_sent, ((wide, 1), (narrow, share), (narrow, share))
    )
    return (
        outputs,
        input_grad.astype(BF),
        query_out,
        key_out,
        value_out,
        output_out,
        gate_out,
        up_out,
        down_out,
        gains[0],
        gains[1],
    )


def solution(mesh):
    return jax.shard_map(
        per_device,
        mesh=mesh,
        in_specs=(
            P("dp", "ctx", "tensor"),
            P("dp", "ctx", "tensor"),
            P(),
            P(),
            P("ctx", "tensor"),
            P("ctx", "tensor"),
            P("ctx", "tensor"),
            P("tensor", "ctx"),
            P("ctx", "tensor"),
            P("ctx", "tensor"),
            P("tensor", "ctx"),
            P("tensor"),
            P("tensor"),
        ),
        out_specs=(
            P("dp", "ctx", "tensor"),
            P("dp", "ctx", "tensor"),
            P(("dp", "ctx"), "tensor"),
            P(("dp", "ctx"), "tensor"),
            P(("dp", "ctx"), "tensor"),
            P("tensor", ("dp", "ctx")),
            P(("dp", "ctx"), "tensor"),
            P(("dp", "ctx"), "tensor"),
            P("tensor", ("dp", "ctx")),
            P("tensor"),
            P("tensor"),
        ),
        check_vma=False,
    )
```

```python
import functools

import jax
import jax.numpy as jnp
from jax import lax
from jax.experimental import pallas as pl
from jax.experimental.pallas import tpu as pltpu
from jax.sharding import PartitionSpec as P

HD = 64
EPS = 1e-05
NEGATIVE = -1e30
BF = jnp.bfloat16


def inverse_frequency(head_size):
    exponent = jnp.arange(0, head_size, 2, dtype=jnp.int32).astype(jnp.float32) / head_size
    plain = 1.0 / jnp.power(jnp.float32(500000.0), exponent)
    factor = 32.0
    old_context = 8192.0
    wavelength = 2.0 * jnp.pi / plain
    smooth = (old_context / wavelength - 1.0) / (4.0 - 1.0)
    scaled = jnp.where(wavelength > old_context, plain / factor, plain)
    middle = (wavelength <= old_context) & (wavelength >= old_context / 4.0)
    scaled = jnp.where(middle, (1.0 - smooth) * plain / factor + smooth * plain, scaled)
    return scaled


def rotation_tables(span):
    positions = jnp.arange(span, dtype=jnp.int32).astype(jnp.float32)
    angle = positions[:, None] * inverse_frequency(HD)[None, :]
    cosine = jnp.cos(angle)
    sine = jnp.sin(angle)
    one = jnp.ones((span, HD), jnp.float32)
    turning = jnp.concatenate([cosine, cosine], axis=1)
    crossing = jnp.concatenate([-sine, sine], axis=1)
    return jnp.stack(
        [
            jnp.concatenate([turning, turning], axis=1),
            jnp.concatenate([crossing, crossing], axis=1),
            jnp.concatenate([turning, one], axis=1),
            jnp.concatenate([crossing, 0.0 * one], axis=1),
        ]
    )


def rotate_lanes(values, tables, rows, sign):
    chunks = values.shape[1] // 128
    lanes = lax.broadcasted_iota(jnp.int32, (values.shape[0], 128), 1)
    first = lanes % HD < HD // 2
    turned = []
    for chunk in range(chunks):
        part = values[:, chunk * 128 : chunk * 128 + 128]
        other = jnp.where(
            first, pltpu.roll(part, 128 - HD // 2, 1), pltpu.roll(part, HD // 2, 1)
        )
        table = 2 if chunk == chunks - 1 else 0
        turned.append(part * tables[table, rows] + sign * other * tables[table + 1, rows])
    return jnp.concatenate(turned, axis=1)


def take_block(here, away, index):
    half = here.shape[1]
    return jnp.where(index < half, here[0, index % half], away[0, index % half])


def put_block(here, away, index, values):
    half = here.shape[1]

    @pl.when(index < half)
    def _():
        here[0, index % half] = values

    @pl.when(index >= half)
    def _():
        away[0, index % half] = values


def split_heads(ref, values, rows, heads):
    for head in range(heads):
        ref[head, rows] = values[:, head * HD : head * HD + HD]


def masked_scores(query, keys, limit):
    scores = lax.dot_general(
        query, keys, (((1,), (1,)), ((), ())), preferred_element_type=jnp.float32
    )
    columns = lax.broadcasted_iota(jnp.int32, scores.shape, 1)
    return jnp.where(columns < limit, scores, NEGATIVE)


def row_limit(start, rows, length):
    positions = start + lax.broadcasted_iota(jnp.int32, (rows, 1), 0)
    return jnp.minimum(positions + 1, length)


def forward_kernel(
    heads,
    order,
    lengths,
    projected_here,
    projected_away,
    tables,
    rotated_here,
    rotated_away,
    attended_here,
    attended_away,
    stats,
    qs,
    ks,
    vs,
):
    _, half, rows, _ = projected_here.shape
    blocks = 2 * half
    wide = heads * HD
    length = lengths[pl.program_id(0)]
    lanes = lax.broadcasted_iota(jnp.int32, (rows, 128), 1)
    for block in range(blocks):
        where = pl.ds(block * rows, rows)
        values = take_block(projected_here, projected_away, order[block])
        turned = rotate_lanes(values, tables, where, 1.0).astype(BF)
        put_block(rotated_here, rotated_away, order[block], turned)
        split_heads(qs, turned[:, :wide] * BF(HD ** (-0.5)), where, heads)
        ks[where] = turned[:, wide : wide + HD]
        vs[where] = turned[:, wide + HD :]
    for block in range(blocks):
        where = pl.ds(block * rows, rows)
        extent = (block + 1) * rows
        limit = row_limit(block * rows, rows, length)
        outs = []
        logs = jnp.zeros((rows, 128), jnp.float32)
        for head in range(heads):
            scores = masked_scores(qs[head, where], ks[:extent], limit)
            top = jnp.max(scores, axis=1, keepdims=True)
            powers = jnp.exp(scores - top)
            total = jnp.sum(powers, axis=1, keepdims=True)
            outs.append((matmul(powers.astype(BF), vs[:extent]) * (1.0 / total)).astype(BF))
            logs = jnp.where(lanes == head, top + jnp.log(total), logs)
        stats[0, where] = logs
        put_block(attended_here, attended_away, order[block], jnp.concatenate(outs, axis=1))


def backward_kernel(
    heads,
    order,
    lengths,
    rotated_here,
    rotated_away,
    grads_here,
    grads_away,
    tables,
    stats,
    back_here,
    back_away,
    qs,
    ks,
    vs,
    gs,
    dqs,
    dks,
    dvs,
):
    _, half, rows, _ = rotated_here.shape
    blocks = 2 * half
    wide = heads * HD
    length = lengths[pl.program_id(0)]
    scale = HD ** (-0.5)
    down = (((0,), (0,)), ((), ()))
    for block in range(blocks):
        where = pl.ds(block * rows, rows)
        turned = take_block(rotated_here, rotated_away, order[block])
        split_heads(qs, turned[:, :wide] * BF(scale), where, heads)
        ks[where] = turned[:, wide : wide + HD]
        vs[where] = turned[:, wide + HD :]
        split_heads(gs, take_block(grads_here, grads_away, order[block]), where, heads)
    dks[...] = jnp.zeros_like(dks)
    dvs[...] = jnp.zeros_like(dvs)
    for block in range(blocks):
        where = pl.ds(block * rows, rows)
        extent = (block + 1) * rows
        limit = row_limit(block * rows, rows, length)
        for head in range(heads):
            query = qs[head, where]
            grad = gs[head, where]
            keys = ks[:extent]
            scores = masked_scores(query, keys, limit)
            probs = jnp.exp(scores - stats[0, where][:, head : head + 1])
            grad_probs = lax.dot_general(
                grad, vs[:extent], (((1,), (1,)), ((), ())), preferred_element_type=jnp.float32
            )
            delta = jnp.sum(probs * grad_probs, axis=1, keepdims=True)
            grad_scores = (probs * (grad_probs - delta)).astype(BF)
            dqs[head, where] = matmul(grad_scores, keys) * scale
            dks[:extent] += lax.dot_general(
                grad_scores, query, down, preferred_element_type=jnp.float32
            )
            dvs[:extent] += lax.dot_general(
                probs.astype(BF), grad, down, preferred_element_type=jnp.float32
            )
    for block in range(blocks):
        where = pl.ds(block * rows, rows)
        parts = [dqs[h, where] for h in range(heads)] + [dks[where], dvs[where]]
        turned = rotate_lanes(jnp.concatenate(parts, axis=1), tables, where, -1.0)
        put_block(back_here, back_away, order[block], turned.astype(BF))


def slot_spec(shape):
    rest = tuple(shape[1:])
    return pl.BlockSpec((1, *rest), lambda slot, *_: (slot,) + (0,) * len(rest))


def attention_call(kernel, heads, order, lengths, tables, arrays, extra, outs, scratch, work):
    slots, half, rows, _ = arrays[0].shape
    span = 2 * half * rows
    return pl.pallas_call(
        functools.partial(kernel, heads),
        grid_spec=pltpu.PrefetchScalarGridSpec(
            num_scalar_prefetch=2,
            grid=(slots,),
            in_specs=[slot_spec(item.shape) for item in arrays]
            + [pl.BlockSpec(tables.shape, lambda slot, *_: (0, 0, 0))]
            + [slot_spec(item.shape) for item in extra],
            out_specs=[slot_spec(item.shape) for item in outs],
            scratch_shapes=scratch,
        ),
        out_shape=outs,
        compiler_params=pltpu.CompilerParams(vmem_limit_bytes=48 * 2**20),
        cost_estimate=pl.CostEstimate(
            flops=work * slots * heads * span * span * HD * 5 // 2,
            bytes_accessed=16 * 2**20,
            transcendentals=slots * heads * span * span,
        ),
    )(order, lengths, *arrays, tables, *extra)


def attention_forward(projected, tables, order, lengths):
    slots, half, rows, columns = projected[0].shape
    heads = columns // HD - 2
    span = 2 * half * rows
    rotated = jax.ShapeDtypeStruct(projected[0].shape, BF)
    attended = jax.ShapeDtypeStruct((slots, half, rows, heads * HD), BF)
    stats = jax.ShapeDtypeStruct((slots, span, 128), jnp.float32)
    scratch = [
        pltpu.VMEM((heads, span, HD), BF),
        pltpu.VMEM((span, HD), BF),
        pltpu.VMEM((span, HD), BF),
    ]
    outs = [rotated, rotated, attended, attended, stats]
    found = attention_call(
        forward_kernel, heads, order, lengths, tables, projected, [], outs, scratch, 4
    )
    return tuple(found[:2]), tuple(found[2:4]), found[4]


def attention_backward(rotated, grads, stats, tables, order, lengths):
    slots, half, rows, columns = rotated[0].shape
    heads = columns // HD - 2
    span = 2 * half * rows
    scratch = [
        pltpu.VMEM((heads, span, HD), BF),
        pltpu.VMEM((span, HD), BF),
        pltpu.VMEM((span, HD), BF),
        pltpu.VMEM((heads, span, HD), BF),
        pltpu.VMEM((heads, span, HD), jnp.float32),
        pltpu.VMEM((span, HD), jnp.float32),
        pltpu.VMEM((span, HD), jnp.float32),
    ]
    outs = [jax.ShapeDtypeStruct(rotated[0].shape, BF)] * 2
    arrays = [*rotated, *grads]
    return attention_call(
        backward_kernel, heads, order, lengths, tables, arrays, [stats], outs, scratch, 10
    )


def matmul(left, right):
    return jnp.dot(left, right, preferred_element_type=jnp.float32)


class Plan:
    def __init__(self, slots):
        self.place = lax.axis_index("ctx")
        self.side = lax.axis_index("tensor")
        self.group = lax.axis_index("dp")
        self.parts = lax.axis_size("ctx")
        self.sides = lax.axis_size("tensor")
        self.groups = lax.axis_size("dp")
        self.fast = self.parts == 4 and self.sides == 2 and self.groups == 4 and slots == 2

    def storage(self):
        members = jnp.arange(self.parts, dtype=jnp.int32)
        if not self.fast:
            return members
        apart = self.place ^ members
        return (apart % 2) * 2 + apart // 2

    def members(self, away):
        half = self.parts // 2
        if not self.fast:
            return jnp.arange(half, dtype=jnp.int32) + away * half
        return self.place ^ (2 * jnp.arange(half, dtype=jnp.int32) + away)

    def ordered(self, block, count):
        return block ^ (self.side * (count // 2)) if self.fast else block


def after(values, anchor):
    return lax.optimization_barrier((values, anchor))[0]


def swap(values, axis, mask):
    size = lax.axis_size(axis)
    return lax.ppermute(values, axis, [(i, i ^ mask) for i in range(size)])


def gather_open(plan, values):
    if not plan.fast:
        wide = lax.all_gather(values, "tensor", axis=2, tiled=True)
        return (lax.all_gather(wide, "ctx", axis=0),)
    zero, one = values[0], values[1]
    zero_side = swap(zero, "tensor", 1)
    one_ctx = swap(one, "ctx", 2)
    zero_ctx = swap(zero, "ctx", 2)
    one_side = swap(one, "tensor", 1)
    zero_far = swap(zero_side, "ctx", 2)
    one_far = swap(one_ctx, "tensor", 1)
    return zero, zero_side, zero_ctx, zero_far, one, one_side, one_ctx, one_far


def aside_open(plan, values):
    if not plan.fast:
        return gather_open(plan, values)
    return values, swap(values, "tensor", 1), swap(values, "ctx", 2)


def aside_turn(plan, opened):
    return (*opened, swap(opened[2], "tensor", 1)) if plan.fast else opened


def gather_close(plan, opened, finish=None):
    if finish is None:
        finish = [lambda half: half] * 2
    if not plan.fast:
        half = plan.parts // 2
        whole = opened[0].swapaxes(0, 1)
        return finish[0](whole[:, :half]), finish[1](whole[:, half:])
    opened = lax.optimization_barrier(opened)
    if len(opened) == 4:
        values, side, ctx, far = opened
        near = jnp.concatenate([values, side], axis=2)
        here = jnp.stack([near, jnp.concatenate([ctx, far], axis=2)], axis=1)
        here = finish[0](here)
        return here, swap(here, "ctx", 1)
    zero, zero_side, zero_ctx, zero_far, one, one_side, one_ctx, one_far = opened
    rows = [
        jnp.concatenate(pair, axis=1)
        for pair in ((zero, zero_side), (zero_ctx, zero_far), (one, one_side), (one_ctx, one_far))
    ]
    here = finish[0](jnp.stack(rows).reshape(2, 2, *rows[0].shape))
    return here, swap(here, "ctx", 1)


def flat(halves):
    return tuple(half.reshape(-1, half.shape[-1]) for half in halves)


def gather_rows(plan, values):
    return flat(gather_close(plan, gather_open(plan, values)))


def wide_sum(*terms):
    return sum(term.astype(jnp.float32) for term in terms)


def scatter_open(plan, lefts, right, slots):
    away = matmul(lefts[1], right).astype(BF)
    here = matmul(lefts[0], right).astype(BF)
    return scatter_halves(plan, here, away, slots)


def scatter_halves(plan, here, away, slots):
    width = here.shape[-1]
    half = plan.parts // 2
    here = here.reshape(slots, half, -1, width)
    away = away.reshape(slots, half, -1, width)
    if not plan.fast:
        return (jnp.concatenate([here, away], axis=1),)
    got = swap(away, "ctx", 1)
    own = width // 2
    zero_sent = wide_sum(here[0, 1], got[0, 1]).astype(BF)
    one_sent = wide_sum(here[1, :, :, own:], got[1, :, :, own:]).astype(BF)
    return here, got, zero_sent, one_sent


def scatter_turn(plan, opened):
    if not plan.fast:
        return opened
    here, got, zero_sent, one_sent = opened
    return here, got, swap(zero_sent, "ctx", 2), swap(one_sent, "tensor", 1)


def scatter_end(plan, turned):
    if not plan.fast:
        whole = turned[0].swapaxes(0, 1)
        narrow = lax.psum_scatter(whole, "tensor", scatter_dimension=3, tiled=True)
        return lax.psum_scatter(narrow, "ctx", scatter_dimension=0, tiled=False).astype(jnp.float32)
    here, got, zero, one = turned
    own = here.shape[-1] // 2
    zero_sent = wide_sum(here[0, 0, :, own:], got[0, 0, :, own:], zero[:, own:]).astype(BF)
    one_sent = wide_sum(here[1, 1, :, :own], got[1, 1, :, :own], one[1]).astype(BF)
    zero_sent, one_sent = lax.optimization_barrier((zero_sent, one_sent))
    zero_last, one_last = lax.optimization_barrier(
        (swap(zero_sent, "tensor", 1), swap(one_sent, "ctx", 2))
    )
    zero_total = wide_sum(here[0, 0, :, :own], got[0, 0, :, :own], zero[:, :own], zero_last)
    one_total = wide_sum(here[1, 0, :, :own], got[1, 0, :, :own], one[0], one_last)
    return jnp.stack([zero_total, one_total])


def scatter_close(plan, opened, beside=None):
    turned = scatter_turn(plan, opened)
    if beside is not None:
        turned = after(turned, beside)
    return scatter_end(plan, turned)


def exchange_pieces(plan, piece):
    found = [piece(plan.place)]
    for mask in range(1, plan.parts):
        found.append(swap(piece(plan.place ^ mask), "ctx", mask))
    return found


def shared_pieces(plan, piece, anchor):
    if not plan.fast:
        return exchange_pieces(plan, piece)
    got = []
    for mask in (2, 3):
        mine = piece(plan.place ^ mask)
        size = mine.shape[0] // plan.groups
        mine = lax.dynamic_slice_in_dim(mine, plan.group * size, size, 0)
        got.append(swap(after(mine, anchor), "ctx", mask))
    return jnp.stack(got)


def shared_close(plan, shared, piece, anchor):
    if not plan.fast:
        return [(item, None) for item in shared]
    whole = lax.all_gather(shared, "dp")
    core = swap(after(piece(plan.place ^ 1), anchor), "ctx", 1)
    return [(piece(plan.place), None), (core, None), (whole, 0), (whole, 1)]


def place_rows(plan, found):
    rows, columns = found[0].shape
    whole = jnp.zeros((rows * plan.parts, columns), found[0].dtype)
    for mask, piece in enumerate(found):
        start = plan.ordered(plan.place ^ mask, plan.parts) * rows
        whole = lax.dynamic_update_slice(whole, piece, (start, 0))
    return whole


def place_columns(plan, found):
    rows, columns = found[0].shape
    whole = jnp.zeros((rows, columns * plan.parts), found[0].dtype)
    for mask, piece in enumerate(found):
        start = plan.ordered(plan.place ^ mask, plan.parts) * columns
        whole = lax.dynamic_update_slice(whole, piece, (0, start))
    return whole


def by_member(plan, found):
    bit = 1
    while bit < plan.parts:
        flip = (plan.place & bit) != 0
        found = [jnp.where(flip, found[i ^ bit], found[i]) for i in range(plan.parts)]
        bit *= 2
    return found


def column_piece(weights, parts, least=1):
    def piece(member):
        taken = []
        for weight in weights:
            share = max(1, least * parts // weight.shape[1])
            size = weight.shape[1] * share // parts
            taken.append(lax.dynamic_slice_in_dim(weight, member // share * size, size, 1))
        return jnp.concatenate(taken, axis=1)

    return piece


def row_piece(weight, parts):
    size = weight.shape[0] // parts

    def piece(member):
        return lax.dynamic_slice_in_dim(weight, member * size, size, 0)

    return piece


def put_rows(places, pieces, whole):
    rows = whole.shape[0] // len(pieces)
    for mask, piece in enumerate(pieces):
        start = pl.multiple_of(places[mask] * rows, rows)
        whole[pl.ds(start, rows)] = piece[...].reshape(rows, whole.shape[1])


def put_columns(places, pieces, whole):
    columns = whole.shape[1] // len(pieces)
    for mask, piece in enumerate(pieces):
        start = pl.multiple_of(places[mask] * columns, columns)
        whole[:, pl.ds(start, columns)] = piece[...]


def forward_units_kernel(places, normed, *refs):
    pieces, (active, slope_gate, slope_up, weights) = refs[:-4], refs[-4:]
    pl.when(pl.program_id(0) == 0)(lambda: put_rows(places, pieces, weights))
    units = weights.shape[1] // 2
    gate = matmul(normed[...], weights[:, :units])
    upward = matmul(normed[...], weights[:, units:])
    sigmoid = jax.nn.sigmoid(gate)
    swish = gate * sigmoid
    active[...] = (swish * upward).astype(BF)
    slope_gate[...] = (upward * sigmoid * (1.0 + gate * (1.0 - sigmoid))).astype(BF)
    slope_up[...] = swish.astype(BF)


def backward_units_kernel(places, target, slope_gate, slope_up, *refs):
    pieces, (grads, back, weights, down) = refs[:-4], refs[-4:]
    half = len(pieces) // 2

    @pl.when(pl.program_id(0) == 0)
    def _():
        put_rows(places, pieces[:half], weights)
        put_columns(places, pieces[half:], down)

    units = down.shape[0]
    across = (((1,), (1,)), ((), ()))
    grad = lax.dot_general(target[...], down[...], across, preferred_element_type=jnp.float32)
    grads[:, :units] = (grad * slope_gate[...]).astype(BF)
    grads[:, units:] = (grad * slope_up[...]).astype(BF)
    total = lax.dot_general(grads[...], weights[...], across, preferred_element_type=jnp.float32)
    back[...] = total.astype(BF)


def whole_spec(array, index):
    once = pl.Buffered(1)
    if index is None:
        return pl.BlockSpec(array.shape, lambda i, _: (0, 0), pipeline_mode=once)
    groups, _, rows, columns = array.shape
    return pl.BlockSpec(
        (groups, 1, rows, columns), lambda i, _: (0, index, 0, 0), pipeline_mode=once
    )


def row_blocks(kernel, places, blocked, pieces, widths, scratch):
    lines = blocked[0].shape[0]
    rows = min(512, lines)
    flops = sum(2 * lines * a * b for a, b in scratch)
    moved = sum(2 * lines * item.shape[1] for item in blocked) + sum(2 * lines * w for w in widths)
    return pl.pallas_call(
        kernel,
        grid_spec=pltpu.PrefetchScalarGridSpec(
            num_scalar_prefetch=1,
            grid=(lines // rows,),
            in_specs=[pl.BlockSpec((rows, item.shape[1]), lambda i, _: (i, 0)) for item in blocked]
            + [whole_spec(*piece) for piece in pieces],
            out_specs=[pl.BlockSpec((rows, width), lambda i, _: (i, 0)) for width in widths],
            scratch_shapes=[pltpu.VMEM(shape, BF) for shape in scratch],
        ),
        out_shape=[jax.ShapeDtypeStruct((lines, width), BF) for width in widths],
        compiler_params=pltpu.CompilerParams(vmem_limit_bytes=58 * 2**20),
        cost_estimate=pl.CostEstimate(
            flops=flops,
            bytes_accessed=moved + sum(2 * a * b for a, b in scratch),
            transcendentals=0,
        ),
    )(places, *blocked, *[array for array, _ in pieces])


def forward_units(places, normed, pieces):
    both = pieces[0][0].shape[1]
    shape = (normed.shape[1], both)
    return row_blocks(forward_units_kernel, places, [normed], pieces, [both // 2] * 3, [shape])


def backward_units(places, target, slopes, pieces, down):
    both = pieces[0][0].shape[1]
    width = target.shape[1]
    return row_blocks(
        backward_units_kernel,
        places,
        [target, *slopes],
        pieces + [(item, None) for item in down],
        [both, width],
        [(width, both), (both // 2, width)],
    )


def gradient_kernel(side, left_here, left_away, right_here, right_away, out):
    total = None
    for left, right in ((left_here, right_here), (left_away, right_away)):
        term = lax.dot_general(
            left[...], right[...], (((0,), (0,)), ((), ())), preferred_element_type=jnp.float32
        )
        total = term if total is None else total + term
    out[...] = total.astype(out.dtype).reshape(out.shape)


def weight_gradient(plan, lefts, rights, features_first, part=0, parts=1):
    tokens, height = lefts[0].shape
    width = rights[0].shape[1] // parts
    groups = plan.groups
    flip = groups // 2 if plan.fast else 0
    tall = height // groups if features_first else height
    broad = width if features_first else width // groups
    step = min(broad, 1024)
    lines = min(tall, 512)
    skip = part * (width // step)

    def at(i, j, side):
        group, line = (i // (tall // lines), i % (tall // lines)) if features_first else (j, i)
        column = j if features_first else 0
        return (group + flip * side[0]) % groups, line, column

    return pl.pallas_call(
        gradient_kernel,
        grid_spec=pltpu.PrefetchScalarGridSpec(
            num_scalar_prefetch=1,
            grid=(height // lines, width // step),
            in_specs=[pl.BlockSpec((tokens, lines), lambda i, j, side: (0, i))] * 2
            + [pl.BlockSpec((tokens, step), lambda i, j, side: (0, j + skip))] * 2,
            out_specs=pl.BlockSpec((1, lines, step), at),
        ),
        out_shape=jax.ShapeDtypeStruct((groups, tall, broad), BF),
        compiler_params=pltpu.CompilerParams(vmem_limit_bytes=48 * 2**20),
        cost_estimate=pl.CostEstimate(
            flops=4 * tokens * height * width,
            bytes_accessed=2 * (2 * tokens * (height + width) + height * width),
            transcendentals=0,
        ),
    )(plan.side[None].astype(jnp.int32), *lefts, *rights)


def reduce_groups(grad):
    return lax.psum_scatter(grad, "dp", scatter_dimension=0)


def reduce_both(plan, left, right):
    rows, columns = left.shape[1:]
    if not plan.fast or 2 * rows != right.shape[1]:
        return reduce_groups(left), reduce_groups(right)
    half = columns // 2
    folded = jnp.concatenate([left[:, :, :half], left[:, :, half:]], axis=1)
    both = reduce_groups(jnp.concatenate([folded, right], axis=2))
    left = jnp.concatenate([both[:rows, :half], both[rows:, :half]], axis=1)
    return left, both[:, half:]


def finish_columns(plan, found, widths):
    found = by_member(plan, found)
    outs = []
    start = 0
    for width, share in widths:
        blocks = [piece[:, start : start + width].astype(jnp.float32) for piece in found]
        blocks = [sum(blocks[i : i + share]) for i in range(0, plan.parts, share)]
        outs.append(jnp.concatenate(blocks, axis=1))
        start += width
    return outs


def finish_rows(plan, found):
    return jnp.concatenate(by_member(plan, found), axis=0).astype(jnp.float32)


def send_rows(plan, part):
    return exchange_pieces(plan, row_piece(part, plan.parts))


def send_columns(plan, part):
    return exchange_pieces(plan, column_piece([part], plan.parts))


def total_over(values, axis):
    others = [swap(values, axis, mask) for mask in range(1, lax.axis_size(axis))]
    return sum(lax.optimization_barrier(others), values)


def feature_total(values):
    total = jnp.sum(values, axis=-1, keepdims=True)
    if lax.axis_size("tensor") == 2:
        return total + swap(total, "tensor", 1)
    return lax.psum(total, "tensor")


def per_device(
    inputs,
    cotangent,
    lengths,
    deal_order,
    query_weight,
    key_weight,
    value_weight,
    output_weight,
    gate_weight,
    up_weight,
    down_weight,
    attention_gain,
    feedforward_gain,
):
    slots, rows, half_width = inputs.shape
    plan = Plan(slots)
    width = half_width * plan.sides
    parts = plan.parts
    groups = plan.groups
    sequences = lengths.shape[0]
    ids = jnp.arange(sequences, dtype=jnp.int32)
    own_ids = plan.group * slots + jnp.arange(slots, dtype=jnp.int32)
    slot_lengths = lax.dynamic_slice_in_dim(lengths, plan.group * slots, slots)
    dealt = jnp.sum(jnp.where(deal_order[:, None] == ids[None, :], lengths[None, :], 0), axis=1)
    totals = jnp.sum(dealt.reshape(groups, -1), axis=1)
    found = jnp.where(deal_order[None, :] == own_ids[:, None], ids[None, :], 0)
    owner = jnp.sum(found, axis=1) // (sequences // groups)
    mine = owner[:, None] == jnp.arange(groups, dtype=jnp.int32)[None, :]
    own_totals = jnp.sum(jnp.where(mine, totals[None, :], 0), axis=1)
    scale = jnp.sum(lengths).astype(jnp.float32) / groups / own_totals.astype(jnp.float32)

    own_rows = plan.place * rows + jnp.arange(rows, dtype=jnp.int32)
    own_valid = own_rows[None, :] < slot_lengths[:, None]
    tables = rotation_tables(parts * rows)
    order = plan.storage()

    def scaled(away):
        starts = plan.members(away) * rows
        positions = starts[:, None] + jnp.arange(rows, dtype=jnp.int32)[None, :]
        valid = positions[None] < slot_lengths[:, None, None]
        factor = jnp.where(valid, scale[:, None, None], 0.0)
        return lambda half: (half.astype(jnp.float32) * factor[..., None]).astype(BF)

    source = inputs.astype(jnp.float32)
    inverse_one = lax.rsqrt(feature_total(source * source) / width + EPS)
    opened = gather_open(plan, (source * inverse_one * attention_gain).astype(BF))
    qkv_w = place_rows(
        plan,
        exchange_pieces(plan, column_piece([query_weight, key_weight, value_weight], parts, HD)),
    )
    normed = gather_close(plan, after(opened, (tables, qkv_w)))
    o_found = exchange_pieces(plan, row_piece(after(output_weight, normed[0]), parts))
    normed = flat(normed)

    wide = query_weight.shape[1] // parts
    share = max(1, HD * parts // key_weight.shape[1])
    narrow = key_weight.shape[1] * share // parts
    half_shape = (slots, parts // 2, rows, -1)
    projected = [matmul(item, qkv_w).reshape(half_shape) for item in normed]
    pair_piece = column_piece([gate_weight, up_weight], parts)
    shared = shared_pieces(plan, pair_piece, projected[1])
    rotated, attended, stats = attention_forward(projected, tables, order, slot_lengths)
    attended = flat(attended)
    attended, o_found, shared = after((attended, o_found, shared), rotated)
    o_w = place_columns(plan, o_found)
    opened = scatter_open(plan, attended, o_w, slots)
    hidden = source + scatter_close(plan, opened)

    inverse_two = lax.rsqrt(feature_total(hidden * hidden) / width + EPS)
    opened = gather_open(plan, (hidden * inverse_two * feedforward_gain).astype(BF))
    pair_w = shared_close(plan, shared, pair_piece, hidden)
    opened, pair_arrays = after((opened, [item for item, _ in pair_w]), hidden)
    pair_w = [(item, index) for item, (_, index) in zip(pair_arrays, pair_w)]
    normed_two = flat(gather_close(plan, opened))
    down_found = exchange_pieces(plan, row_piece(after(down_weight, normed_two[0]), parts))
    target_open = aside_open(plan, after(cotangent, normed_two[0]))
    units = gate_weight.shape[1] // parts
    masks = jnp.arange(parts, dtype=jnp.int32)
    places = plan.ordered(plan.place ^ masks, parts)
    active_here, *slopes_here = forward_units(places, normed_two[0], pair_w)
    away, target_open = after((normed_two[1], target_open), active_here)
    normed_two = (normed_two[0], away)
    target_open = aside_turn(plan, target_open)
    active_away, *slopes_away = forward_units(places, normed_two[1], pair_w)
    active = (active_here, active_away)
    active, target_open, down_found[:3] = after((active, target_open, down_found[:3]), active_away)
    target_all = flat(gather_close(plan, target_open, [scaled(0), scaled(1)]))
    target_all, down_found[3:] = after((target_all, down_found[3:]), active)
    down_sum = weight_gradient(plan, active, target_all, False)
    down_part = reduce_groups(down_sum)

    target = cotangent.astype(jnp.float32) * own_valid[:, :, None] * scale[:, None, None]
    target_away = after(target_all[1], down_sum)
    grads_away, away = backward_units(places, target_away, slopes_away, pair_w, down_found)
    target_here = after(target_all[0], away)
    grads_here, here = backward_units(places, target_here, slopes_here, pair_w, down_found)
    grad_pair = (grads_here, grads_away)
    opened = scatter_halves(plan, here, away, slots)
    grad_late = after(grad_pair, opened[-1])
    gate_sum = weight_gradient(plan, normed_two, grad_late, True, 0, 2)
    gate_part = reduce_groups(gate_sum)
    dn = scatter_close(plan, opened, (gate_sum, down_part))
    weighted = dn * feedforward_gain
    total_two = feature_total(weighted * hidden)
    grad_hidden = target + inverse_two * weighted - hidden * inverse_two**3 * total_two / width
    gain_two_sum = jnp.sum(dn * hidden * inverse_two, axis=(0, 1))

    down_w = place_columns(plan, after(down_found, dn))
    result_open = scatter_open(plan, after(active, grad_hidden), down_w, slots)
    up_sum = weight_gradient(plan, normed_two, after(grad_pair, grad_hidden), True, 1, 2)
    up_part = reduce_groups(up_sum)
    opened = after(gather_open(plan, grad_hidden.astype(BF)), (result_open, up_sum, gate_part))
    grad_hidden_all = flat(gather_close(plan, opened))
    result_open, down_part, gate_part = after((result_open, down_part, gate_part), grad_hidden_all)
    result_turned = scatter_turn(plan, result_open)
    down_sent = send_columns(plan, down_part)
    gate_sent = send_rows(plan, gate_part)
    grad_attended = [matmul(item, o_w.T).astype(BF) for item in grad_hidden_all]
    output_sum = weight_gradient(plan, attended, grad_hidden_all, False)
    grad_attended = after(grad_attended, output_sum)
    grad_attended = [item.reshape(half_shape) for item in grad_attended]
    back = attention_backward(rotated, grad_attended, stats, tables, order, slot_lengths)
    sent = (result_turned, down_sent, gate_sent, output_sum)
    back, sent = after((flat(back), sent), back)
    result_turned, down_sent, gate_sent, output_sum = sent
    opened = scatter_open(plan, back, qkv_w.T, slots)
    qkv_sum = weight_gradient(plan, normed, after(back, opened[-1]), True)
    result = hidden + scatter_end(plan, result_turned)
    outputs = jnp.where(own_valid[:, :, None], result, 0.0).astype(BF)
    output_part, qkv_part = reduce_both(plan, output_sum, qkv_sum)
    dm = scatter_close(plan, opened, (qkv_sum, up_part, outputs))
    up_part = after(up_part, dm)
    up_sent = send_rows(plan, up_part)
    flip = plan.side * (width // 2) if plan.fast else 0
    halves = jnp.sum(
        jnp.roll(qkv_sum.reshape(width, -1).astype(jnp.float32), flip, 0)
        * qkv_w.astype(jnp.float32),
        axis=1,
    )
    if plan.fast:
        gain_one_sum = halves[:half_width] + after(swap(halves[half_width:], "tensor", 1), dm)
    else:
        gain_one_sum = lax.psum_scatter(halves, "tensor", scatter_dimension=0, tiled=True)
    gain_one_sum = gain_one_sum / attention_gain
    weighted = dm * attention_gain
    total_one = feature_total(weighted * source)
    input_grad = grad_hidden + inverse_one * weighted - source * inverse_one**3 * total_one / width

    gains = total_over(total_over(jnp.stack([gain_one_sum, gain_two_sum]), "ctx"), "dp")
    output_part, qkv_part = after((output_part, qkv_part), gains)
    output_sent = send_columns(plan, output_part)
    qkv_sent = send_rows(plan, qkv_part)
    down_out = finish_rows(plan, down_sent)
    (gate_out,) = finish_columns(plan, gate_sent, ((units, 1),))
    (up_out,) = finish_columns(plan, up_sent, ((units, 1),))
    output_out = finish_rows(plan, output_sent)
    query_out, key_out, value_out = finish_columns(
        plan, qkv_sent, ((wide, 1), (narrow, share), (narrow, share))
    )
    return (
        outputs,
        input_grad.astype(BF),
        query_out,
        key_out,
        value_out,
        output_out,
        gate_out,
        up_out,
        down_out,
        gains[0],
        gains[1],
    )


def solution(mesh):
    return jax.shard_map(
        per_device,
        mesh=mesh,
        in_specs=(
            P("dp", "ctx", "tensor"),
            P("dp", "ctx", "tensor"),
            P(),
            P(),
            P("ctx", "tensor"),
            P("ctx", "tensor"),
            P("ctx", "tensor"),
            P("tensor", "ctx"),
            P("ctx", "tensor"),
            P("ctx", "tensor"),
            P("tensor", "ctx"),
            P("tensor"),
            P("tensor"),
        ),
        out_specs=(
            P("dp", "ctx", "tensor"),
            P("dp", "ctx", "tensor"),
            P(("dp", "ctx"), "tensor"),
            P(("dp", "ctx"), "tensor"),
            P(("dp", "ctx"), "tensor"),
            P("tensor", ("dp", "ctx")),
            P(("dp", "ctx"), "tensor"),
            P(("dp", "ctx"), "tensor"),
            P("tensor", ("dp", "ctx")),
            P("tensor"),
            P("tensor"),
        ),
        check_vma=False,
    )
```

```python
import functools

import jax
import jax.numpy as jnp
from jax import lax
from jax.experimental import pallas as pl
from jax.experimental.pallas import tpu as pltpu
from jax.sharding import PartitionSpec as P

HD = 64
EPS = 1e-05
NEGATIVE = -1e30
BF = jnp.bfloat16


def inverse_frequency(head_size):
    exponent = jnp.arange(0, head_size, 2, dtype=jnp.int32).astype(jnp.float32) / head_size
    plain = 1.0 / jnp.power(jnp.float32(500000.0), exponent)
    factor = 32.0
    old_context = 8192.0
    wavelength = 2.0 * jnp.pi / plain
    smooth = (old_context / wavelength - 1.0) / (4.0 - 1.0)
    scaled = jnp.where(wavelength > old_context, plain / factor, plain)
    middle = (wavelength <= old_context) & (wavelength >= old_context / 4.0)
    scaled = jnp.where(middle, (1.0 - smooth) * plain / factor + smooth * plain, scaled)
    return scaled


def rotation_tables(span):
    positions = jnp.arange(span, dtype=jnp.int32).astype(jnp.float32)
    angle = positions[:, None] * inverse_frequency(HD)[None, :]
    cosine = jnp.cos(angle)
    sine = jnp.sin(angle)
    one = jnp.ones((span, HD), jnp.float32)
    turning = jnp.concatenate([cosine, cosine], axis=1)
    crossing = jnp.concatenate([-sine, sine], axis=1)
    return jnp.stack(
        [
            jnp.concatenate([turning, turning], axis=1),
            jnp.concatenate([crossing, crossing], axis=1),
            jnp.concatenate([turning, one], axis=1),
            jnp.concatenate([crossing, 0.0 * one], axis=1),
        ]
    )


def rotate_lanes(values, tables, rows, sign):
    chunks = values.shape[1] // 128
    lanes = lax.broadcasted_iota(jnp.int32, (values.shape[0], 128), 1)
    first = lanes % HD < HD // 2
    turned = []
    for chunk in range(chunks):
        part = values[:, chunk * 128 : chunk * 128 + 128]
        other = jnp.where(
            first, pltpu.roll(part, 128 - HD // 2, 1), pltpu.roll(part, HD // 2, 1)
        )
        table = 2 if chunk == chunks - 1 else 0
        turned.append(part * tables[table, rows] + sign * other * tables[table + 1, rows])
    return jnp.concatenate(turned, axis=1)


def take_block(here, away, index):
    half = here.shape[1]
    return jnp.where(index < half, here[0, index % half], away[0, index % half])


def put_block(here, away, index, values):
    half = here.shape[1]

    @pl.when(index < half)
    def _():
        here[0, index % half] = values

    @pl.when(index >= half)
    def _():
        away[0, index % half] = values


def split_heads(ref, values, rows, heads):
    for head in range(heads):
        ref[head, rows] = values[:, head * HD : head * HD + HD]


def masked_scores(query, keys, limit):
    scores = lax.dot_general(
        query, keys, (((1,), (1,)), ((), ())), preferred_element_type=jnp.float32
    )
    columns = lax.broadcasted_iota(jnp.int32, scores.shape, 1)
    return jnp.where(columns < limit, scores, NEGATIVE)


def row_limit(start, rows, length):
    positions = start + lax.broadcasted_iota(jnp.int32, (rows, 1), 0)
    return jnp.minimum(positions + 1, length)


def forward_kernel(
    heads,
    order,
    lengths,
    projected_here,
    projected_away,
    tables,
    rotated_here,
    rotated_away,
    attended_here,
    attended_away,
    stats,
    qs,
    ks,
    vs,
):
    _, half, rows, _ = projected_here.shape
    blocks = 2 * half
    wide = heads * HD
    length = lengths[pl.program_id(0)]
    lanes = lax.broadcasted_iota(jnp.int32, (rows, 128), 1)
    for block in range(blocks):
        where = pl.ds(block * rows, rows)
        values = take_block(projected_here, projected_away, order[block])
        turned = rotate_lanes(values, tables, where, 1.0).astype(BF)
        put_block(rotated_here, rotated_away, order[block], turned)
        split_heads(qs, turned[:, :wide] * BF(HD ** (-0.5)), where, heads)
        ks[where] = turned[:, wide : wide + HD]
        vs[where] = turned[:, wide + HD :]
    for block in range(blocks):
        where = pl.ds(block * rows, rows)
        extent = (block + 1) * rows
        limit = row_limit(block * rows, rows, length)
        outs = []
        logs = jnp.zeros((rows, 128), jnp.float32)
        for head in range(heads):
            scores = masked_scores(qs[head, where], ks[:extent], limit)
            top = jnp.max(scores, axis=1, keepdims=True)
            powers = jnp.exp(scores - top)
            total = jnp.sum(powers, axis=1, keepdims=True)
            outs.append((matmul(powers.astype(BF), vs[:extent]) * (1.0 / total)).astype(BF))
            logs = jnp.where(lanes == head, top + jnp.log(total), logs)
        stats[0, where] = logs
        put_block(attended_here, attended_away, order[block], jnp.concatenate(outs, axis=1))


def backward_kernel(
    heads,
    order,
    lengths,
    rotated_here,
    rotated_away,
    grads_here,
    grads_away,
    tables,
    stats,
    back_here,
    back_away,
    qs,
    ks,
    vs,
    gs,
    dqs,
    dks,
    dvs,
):
    _, half, rows, _ = rotated_here.shape
    blocks = 2 * half
    wide = heads * HD
    length = lengths[pl.program_id(0)]
    scale = HD ** (-0.5)
    down = (((0,), (0,)), ((), ()))
    for block in range(blocks):
        where = pl.ds(block * rows, rows)
        turned = take_block(rotated_here, rotated_away, order[block])
        split_heads(qs, turned[:, :wide] * BF(scale), where, heads)
        ks[where] = turned[:, wide : wide + HD]
        vs[where] = turned[:, wide + HD :]
        split_heads(gs, take_block(grads_here, grads_away, order[block]), where, heads)
    dks[...] = jnp.zeros_like(dks)
    dvs[...] = jnp.zeros_like(dvs)
    for block in range(blocks):
        where = pl.ds(block * rows, rows)
        extent = (block + 1) * rows
        limit = row_limit(block * rows, rows, length)
        for head in range(heads):
            query = qs[head, where]
            grad = gs[head, where]
            keys = ks[:extent]
            scores = masked_scores(query, keys, limit)
            probs = jnp.exp(scores - stats[0, where][:, head : head + 1])
            grad_probs = lax.dot_general(
                grad, vs[:extent], (((1,), (1,)), ((), ())), preferred_element_type=jnp.float32
            )
            delta = jnp.sum(probs * grad_probs, axis=1, keepdims=True)
            grad_scores = (probs * (grad_probs - delta)).astype(BF)
            dqs[head, where] = matmul(grad_scores, keys) * scale
            dks[:extent] += lax.dot_general(
                grad_scores, query, down, preferred_element_type=jnp.float32
            )
            dvs[:extent] += lax.dot_general(
                probs.astype(BF), grad, down, preferred_element_type=jnp.float32
            )
    for block in range(blocks):
        where = pl.ds(block * rows, rows)
        parts = [dqs[h, where] for h in range(heads)] + [dks[where], dvs[where]]
        turned = rotate_lanes(jnp.concatenate(parts, axis=1), tables, where, -1.0)
        put_block(back_here, back_away, order[block], turned.astype(BF))


def slot_spec(shape):
    rest = tuple(shape[1:])
    return pl.BlockSpec((1, *rest), lambda slot, *_: (slot,) + (0,) * len(rest))


def attention_call(kernel, heads, order, lengths, tables, arrays, extra, outs, scratch, work):
    slots, half, rows, _ = arrays[0].shape
    span = 2 * half * rows
    return pl.pallas_call(
        functools.partial(kernel, heads),
        grid_spec=pltpu.PrefetchScalarGridSpec(
            num_scalar_prefetch=2,
            grid=(slots,),
            in_specs=[slot_spec(item.shape) for item in arrays]
            + [pl.BlockSpec(tables.shape, lambda slot, *_: (0, 0, 0))]
            + [slot_spec(item.shape) for item in extra],
            out_specs=[slot_spec(item.shape) for item in outs],
            scratch_shapes=scratch,
        ),
        out_shape=outs,
        compiler_params=pltpu.CompilerParams(vmem_limit_bytes=48 * 2**20),
        cost_estimate=pl.CostEstimate(
            flops=work * slots * heads * span * span * HD * 5 // 2,
            bytes_accessed=16 * 2**20,
            transcendentals=slots * heads * span * span,
        ),
    )(order, lengths, *arrays, tables, *extra)


def attention_forward(projected, tables, order, lengths):
    slots, half, rows, columns = projected[0].shape
    heads = columns // HD - 2
    span = 2 * half * rows
    rotated = jax.ShapeDtypeStruct(projected[0].shape, BF)
    attended = jax.ShapeDtypeStruct((slots, half, rows, heads * HD), BF)
    stats = jax.ShapeDtypeStruct((slots, span, 128), jnp.float32)
    scratch = [
        pltpu.VMEM((heads, span, HD), BF),
        pltpu.VMEM((span, HD), BF),
        pltpu.VMEM((span, HD), BF),
    ]
    outs = [rotated, rotated, attended, attended, stats]
    found = attention_call(
        forward_kernel, heads, order, lengths, tables, projected, [], outs, scratch, 4
    )
    return tuple(found[:2]), tuple(found[2:4]), found[4]


def attention_backward(rotated, grads, stats, tables, order, lengths):
    slots, half, rows, columns = rotated[0].shape
    heads = columns // HD - 2
    span = 2 * half * rows
    scratch = [
        pltpu.VMEM((heads, span, HD), BF),
        pltpu.VMEM((span, HD), BF),
        pltpu.VMEM((span, HD), BF),
        pltpu.VMEM((heads, span, HD), BF),
        pltpu.VMEM((heads, span, HD), jnp.float32),
        pltpu.VMEM((span, HD), jnp.float32),
        pltpu.VMEM((span, HD), jnp.float32),
    ]
    outs = [jax.ShapeDtypeStruct(rotated[0].shape, BF)] * 2
    arrays = [*rotated, *grads]
    return attention_call(
        backward_kernel, heads, order, lengths, tables, arrays, [stats], outs, scratch, 10
    )


def matmul(left, right):
    return jnp.dot(left, right, preferred_element_type=jnp.float32)


class Plan:
    def __init__(self, slots):
        self.place = lax.axis_index("ctx")
        self.side = lax.axis_index("tensor")
        self.group = lax.axis_index("dp")
        self.parts = lax.axis_size("ctx")
        self.sides = lax.axis_size("tensor")
        self.groups = lax.axis_size("dp")
        self.fast = self.parts == 4 and self.sides == 2 and self.groups == 4 and slots == 2

    def storage(self):
        members = jnp.arange(self.parts, dtype=jnp.int32)
        if not self.fast:
            return members
        apart = self.place ^ members
        return (apart % 2) * 2 + apart // 2

    def members(self, away):
        half = self.parts // 2
        if not self.fast:
            return jnp.arange(half, dtype=jnp.int32) + away * half
        return self.place ^ (2 * jnp.arange(half, dtype=jnp.int32) + away)

    def ordered(self, block, count):
        return block ^ (self.side * (count // 2)) if self.fast else block


def after(values, anchor):
    return lax.optimization_barrier((values, anchor))[0]


def swap(values, axis, mask):
    size = lax.axis_size(axis)
    return lax.ppermute(values, axis, [(i, i ^ mask) for i in range(size)])


def gather_open(plan, values):
    if not plan.fast:
        wide = lax.all_gather(values, "tensor", axis=2, tiled=True)
        return (lax.all_gather(wide, "ctx", axis=0),)
    zero, one = values[0], values[1]
    zero_side = swap(zero, "tensor", 1)
    one_ctx = swap(one, "ctx", 2)
    zero_ctx = swap(zero, "ctx", 2)
    one_side = swap(one, "tensor", 1)
    zero_far = swap(zero_side, "ctx", 2)
    one_far = swap(one_ctx, "tensor", 1)
    return zero, zero_side, zero_ctx, zero_far, one, one_side, one_ctx, one_far


def aside_open(plan, values):
    if not plan.fast:
        return gather_open(plan, values)
    return values, swap(values, "tensor", 1), swap(values, "ctx", 2)


def aside_turn(plan, opened):
    return (*opened, swap(opened[2], "tensor", 1)) if plan.fast else opened


def gather_close(plan, opened, finish=None):
    if finish is None:
        finish = [lambda half: half] * 2
    if not plan.fast:
        half = plan.parts // 2
        whole = opened[0].swapaxes(0, 1)
        return finish[0](whole[:, :half]), finish[1](whole[:, half:])
    opened = lax.optimization_barrier(opened)
    if len(opened) == 4:
        values, side, ctx, far = opened
        near = jnp.concatenate([values, side], axis=2)
        here = jnp.stack([near, jnp.concatenate([ctx, far], axis=2)], axis=1)
        here = finish[0](here)
        return here, swap(here, "ctx", 1)
    zero, zero_side, zero_ctx, zero_far, one, one_side, one_ctx, one_far = opened
    rows = [
        jnp.concatenate(pair, axis=1)
        for pair in ((zero, zero_side), (zero_ctx, zero_far), (one, one_side), (one_ctx, one_far))
    ]
    here = finish[0](jnp.stack(rows).reshape(2, 2, *rows[0].shape))
    return here, swap(here, "ctx", 1)


def flat(halves):
    return tuple(half.reshape(-1, half.shape[-1]) for half in halves)


def gather_rows(plan, values):
    return flat(gather_close(plan, gather_open(plan, values)))


def wide_sum(*terms):
    return sum(term.astype(jnp.float32) for term in terms)


def scatter_open(plan, lefts, right, slots):
    away = matmul(lefts[1], right).astype(BF)
    here = matmul(lefts[0], right).astype(BF)
    return scatter_halves(plan, here, away, slots)


def scatter_halves(plan, here, away, slots):
    width = here.shape[-1]
    half = plan.parts // 2
    here = here.reshape(slots, half, -1, width)
    away = away.reshape(slots, half, -1, width)
    if not plan.fast:
        return (jnp.concatenate([here, away], axis=1),)
    got = swap(away, "ctx", 1)
    own = width // 2
    zero_sent = wide_sum(here[0, 1], got[0, 1]).astype(BF)
    one_sent = wide_sum(here[1, :, :, own:], got[1, :, :, own:]).astype(BF)
    return here, got, zero_sent, one_sent


def scatter_turn(plan, opened):
    if not plan.fast:
        return opened
    here, got, zero_sent, one_sent = opened
    return here, got, swap(zero_sent, "ctx", 2), swap(one_sent, "tensor", 1)


def scatter_end(plan, turned):
    if not plan.fast:
        whole = turned[0].swapaxes(0, 1)
        narrow = lax.psum_scatter(whole, "tensor", scatter_dimension=3, tiled=True)
        return lax.psum_scatter(narrow, "ctx", scatter_dimension=0, tiled=False).astype(jnp.float32)
    here, got, zero, one = turned
    own = here.shape[-1] // 2
    zero_sent = wide_sum(here[0, 0, :, own:], got[0, 0, :, own:], zero[:, own:]).astype(BF)
    one_sent = wide_sum(here[1, 1, :, :own], got[1, 1, :, :own], one[1]).astype(BF)
    zero_sent, one_sent = lax.optimization_barrier((zero_sent, one_sent))
    zero_last, one_last = lax.optimization_barrier(
        (swap(zero_sent, "tensor", 1), swap(one_sent, "ctx", 2))
    )
    zero_total = wide_sum(here[0, 0, :, :own], got[0, 0, :, :own], zero[:, :own], zero_last)
    one_total = wide_sum(here[1, 0, :, :own], got[1, 0, :, :own], one[0], one_last)
    return jnp.stack([zero_total, one_total])


def scatter_close(plan, opened, beside=None):
    turned = scatter_turn(plan, opened)
    if beside is not None:
        turned = after(turned, beside)
    return scatter_end(plan, turned)


def exchange_pieces(plan, piece):
    found = [piece(plan.place)]
    for mask in range(1, plan.parts):
        found.append(swap(piece(plan.place ^ mask), "ctx", mask))
    return found


def shared_pieces(plan, weights, anchor):
    if not plan.fast:
        return exchange_pieces(plan, column_piece(weights, plan.parts))
    size = weights[0].shape[0] // plan.groups
    lines = [lax.dynamic_slice_in_dim(w, plan.group * size, size, 0) for w in weights]
    piece = column_piece(lines, plan.parts)
    return jnp.stack([swap(after(piece(plan.place ^ m), anchor), "ctx", m) for m in (2, 3)])


def shared_close(plan, shared, piece, anchor):
    if not plan.fast:
        return [(item, None) for item in shared]
    whole = lax.all_gather(shared, "dp")
    core = swap(after(piece(plan.place ^ 1), anchor), "ctx", 1)
    return [(piece(plan.place), None), (core, None), (whole, 0), (whole, 1)]


def place_rows(plan, found):
    rows, columns = found[0].shape
    whole = jnp.zeros((rows * plan.parts, columns), found[0].dtype)
    for mask, piece in enumerate(found):
        start = plan.ordered(plan.place ^ mask, plan.parts) * rows
        whole = lax.dynamic_update_slice(whole, piece, (start, 0))
    return whole


def place_columns(plan, found):
    rows, columns = found[0].shape
    whole = jnp.zeros((rows, columns * plan.parts), found[0].dtype)
    for mask, piece in enumerate(found):
        start = plan.ordered(plan.place ^ mask, plan.parts) * columns
        whole = lax.dynamic_update_slice(whole, piece, (0, start))
    return whole


def by_member(plan, found):
    bit = 1
    while bit < plan.parts:
        flip = (plan.place & bit) != 0
        found = [jnp.where(flip, found[i ^ bit], found[i]) for i in range(plan.parts)]
        bit *= 2
    return found


def column_piece(weights, parts, least=1):
    def piece(member):
        taken = []
        for weight in weights:
            share = max(1, least * parts // weight.shape[1])
            size = weight.shape[1] * share // parts
            taken.append(lax.dynamic_slice_in_dim(weight, member // share * size, size, 1))
        return jnp.concatenate(taken, axis=1)

    return piece


def row_piece(weight, parts):
    size = weight.shape[0] // parts

    def piece(member):
        return lax.dynamic_slice_in_dim(weight, member * size, size, 0)

    return piece


def put_rows(places, pieces, whole):
    rows = whole.shape[0] // len(pieces)
    for mask, piece in enumerate(pieces):
        start = pl.multiple_of(places[mask] * rows, rows)
        whole[pl.ds(start, rows)] = piece[...].reshape(rows, whole.shape[1])


def put_columns(places, pieces, whole):
    columns = whole.shape[1] // len(pieces)
    for mask, piece in enumerate(pieces):
        start = pl.multiple_of(places[mask] * columns, columns)
        whole[:, pl.ds(start, columns)] = piece[...]


def forward_units_kernel(places, normed, *refs):
    pieces, (active, slope_gate, slope_up, weights) = refs[:-4], refs[-4:]
    pl.when(pl.program_id(0) == 0)(lambda: put_rows(places, pieces, weights))
    units = weights.shape[1] // 2
    gate = matmul(normed[...], weights[:, :units])
    upward = matmul(normed[...], weights[:, units:])
    sigmoid = jax.nn.sigmoid(gate)
    swish = gate * sigmoid
    active[...] = (swish * upward).astype(BF)
    slope_gate[...] = (upward * sigmoid * (1.0 + gate * (1.0 - sigmoid))).astype(BF)
    slope_up[...] = swish.astype(BF)


def backward_units_kernel(places, target, slope_gate, slope_up, *refs):
    pieces, (grads, back, weights, down) = refs[:-4], refs[-4:]
    half = len(pieces) // 2

    @pl.when(pl.program_id(0) == 0)
    def _():
        put_rows(places, pieces[:half], weights)
        put_columns(places, pieces[half:], down)

    units = down.shape[0]
    across = (((1,), (1,)), ((), ()))
    grad = lax.dot_general(target[...], down[...], across, preferred_element_type=jnp.float32)
    grads[:, :units] = (grad * slope_gate[...]).astype(BF)
    grads[:, units:] = (grad * slope_up[...]).astype(BF)
    total = lax.dot_general(grads[...], weights[...], across, preferred_element_type=jnp.float32)
    back[...] = total.astype(BF)


def whole_spec(array, index):
    once = pl.Buffered(1)
    if index is None:
        return pl.BlockSpec(array.shape, lambda i, _: (0, 0), pipeline_mode=once)
    groups, _, rows, columns = array.shape
    return pl.BlockSpec(
        (groups, 1, rows, columns), lambda i, _: (0, index, 0, 0), pipeline_mode=once
    )


def row_blocks(kernel, places, blocked, pieces, widths, scratch):
    lines = blocked[0].shape[0]
    rows = min(512, lines)
    flops = sum(2 * lines * a * b for a, b in scratch)
    moved = sum(2 * lines * item.shape[1] for item in blocked) + sum(2 * lines * w for w in widths)
    return pl.pallas_call(
        kernel,
        grid_spec=pltpu.PrefetchScalarGridSpec(
            num_scalar_prefetch=1,
            grid=(lines // rows,),
            in_specs=[pl.BlockSpec((rows, item.shape[1]), lambda i, _: (i, 0)) for item in blocked]
            + [whole_spec(*piece) for piece in pieces],
            out_specs=[pl.BlockSpec((rows, width), lambda i, _: (i, 0)) for width in widths],
            scratch_shapes=[pltpu.VMEM(shape, BF) for shape in scratch],
        ),
        out_shape=[jax.ShapeDtypeStruct((lines, width), BF) for width in widths],
        compiler_params=pltpu.CompilerParams(vmem_limit_bytes=58 * 2**20),
        cost_estimate=pl.CostEstimate(
            flops=flops,
            bytes_accessed=moved + sum(2 * a * b for a, b in scratch),
            transcendentals=0,
        ),
    )(places, *blocked, *[array for array, _ in pieces])


def forward_units(places, normed, pieces):
    both = pieces[0][0].shape[1]
    shape = (normed.shape[1], both)
    return row_blocks(forward_units_kernel, places, [normed], pieces, [both // 2] * 3, [shape])


def backward_units(places, target, slopes, pieces, down):
    both = pieces[0][0].shape[1]
    width = target.shape[1]
    return row_blocks(
        backward_units_kernel,
        places,
        [target, *slopes],
        pieces + [(item, None) for item in down],
        [both, width],
        [(width, both), (both // 2, width)],
    )


def gradient_kernel(side, left_here, left_away, right_here, right_away, out):
    total = None
    for left, right in ((left_here, right_here), (left_away, right_away)):
        term = lax.dot_general(
            left[...], right[...], (((0,), (0,)), ((), ())), preferred_element_type=jnp.float32
        )
        total = term if total is None else total + term
    out[...] = total.astype(out.dtype).reshape(out.shape)


def weight_gradient(plan, lefts, rights, features_first, part=0, parts=1):
    tokens, height = lefts[0].shape
    width = rights[0].shape[1] // parts
    groups = plan.groups
    flip = groups // 2 if plan.fast else 0
    tall = height // groups if features_first else height
    broad = width if features_first else width // groups
    step = min(broad, 1024)
    lines = min(tall, 512)
    skip = part * (width // step)

    def at(i, j, side):
        group, line = (i // (tall // lines), i % (tall // lines)) if features_first else (j, i)
        column = j if features_first else 0
        return (group + flip * side[0]) % groups, line, column

    return pl.pallas_call(
        gradient_kernel,
        grid_spec=pltpu.PrefetchScalarGridSpec(
            num_scalar_prefetch=1,
            grid=(height // lines, width // step),
            in_specs=[pl.BlockSpec((tokens, lines), lambda i, j, side: (0, i))] * 2
            + [pl.BlockSpec((tokens, step), lambda i, j, side: (0, j + skip))] * 2,
            out_specs=pl.BlockSpec((1, lines, step), at),
        ),
        out_shape=jax.ShapeDtypeStruct((groups, tall, broad), BF),
        compiler_params=pltpu.CompilerParams(vmem_limit_bytes=48 * 2**20),
        cost_estimate=pl.CostEstimate(
            flops=4 * tokens * height * width,
            bytes_accessed=2 * (2 * tokens * (height + width) + height * width),
            transcendentals=0,
        ),
    )(plan.side[None].astype(jnp.int32), *lefts, *rights)


def reduce_groups(grad):
    return lax.psum_scatter(grad, "dp", scatter_dimension=0)


def reduce_both(plan, left, right):
    rows, columns = left.shape[1:]
    if not plan.fast or 2 * rows != right.shape[1]:
        return reduce_groups(left), reduce_groups(right)
    half = columns // 2
    folded = jnp.concatenate([left[:, :, :half], left[:, :, half:]], axis=1)
    both = reduce_groups(jnp.concatenate([folded, right], axis=2))
    left = jnp.concatenate([both[:rows, :half], both[rows:, :half]], axis=1)
    return left, both[:, half:]


def finish_columns(plan, found, widths):
    found = by_member(plan, found)
    outs = []
    start = 0
    for width, share in widths:
        blocks = [piece[:, start : start + width].astype(jnp.float32) for piece in found]
        blocks = [sum(blocks[i : i + share]) for i in range(0, plan.parts, share)]
        outs.append(jnp.concatenate(blocks, axis=1))
        start += width
    return outs


def finish_rows(plan, found):
    return jnp.concatenate(by_member(plan, found), axis=0).astype(jnp.float32)


def send_rows(plan, part):
    return exchange_pieces(plan, row_piece(part, plan.parts))


def send_columns(plan, part):
    return exchange_pieces(plan, column_piece([part], plan.parts))


def total_over(values, axis):
    others = [swap(values, axis, mask) for mask in range(1, lax.axis_size(axis))]
    return sum(lax.optimization_barrier(others), values)


def feature_total(values):
    total = jnp.sum(values, axis=-1, keepdims=True)
    if lax.axis_size("tensor") == 2:
        return total + swap(total, "tensor", 1)
    return lax.psum(total, "tensor")


def per_device(
    inputs,
    cotangent,
    lengths,
    deal_order,
    query_weight,
    key_weight,
    value_weight,
    output_weight,
    gate_weight,
    up_weight,
    down_weight,
    attention_gain,
    feedforward_gain,
):
    slots, rows, half_width = inputs.shape
    plan = Plan(slots)
    width = half_width * plan.sides
    parts = plan.parts
    groups = plan.groups
    sequences = lengths.shape[0]
    ids = jnp.arange(sequences, dtype=jnp.int32)
    own_ids = plan.group * slots + jnp.arange(slots, dtype=jnp.int32)
    slot_lengths = lax.dynamic_slice_in_dim(lengths, plan.group * slots, slots)
    dealt = jnp.sum(jnp.where(deal_order[:, None] == ids[None, :], lengths[None, :], 0), axis=1)
    totals = jnp.sum(dealt.reshape(groups, -1), axis=1)
    found = jnp.where(deal_order[None, :] == own_ids[:, None], ids[None, :], 0)
    owner = jnp.sum(found, axis=1) // (sequences // groups)
    mine = owner[:, None] == jnp.arange(groups, dtype=jnp.int32)[None, :]
    own_totals = jnp.sum(jnp.where(mine, totals[None, :], 0), axis=1)
    scale = jnp.sum(lengths).astype(jnp.float32) / groups / own_totals.astype(jnp.float32)

    own_rows = plan.place * rows + jnp.arange(rows, dtype=jnp.int32)
    own_valid = own_rows[None, :] < slot_lengths[:, None]
    tables = rotation_tables(parts * rows)
    order = plan.storage()

    def scaled(away):
        starts = plan.members(away) * rows
        positions = starts[:, None] + jnp.arange(rows, dtype=jnp.int32)[None, :]
        valid = positions[None] < slot_lengths[:, None, None]
        factor = jnp.where(valid, scale[:, None, None], 0.0)
        return lambda half: (half.astype(jnp.float32) * factor[..., None]).astype(BF)

    source = inputs.astype(jnp.float32)
    inverse_one = lax.rsqrt(feature_total(source * source) / width + EPS)
    opened = gather_open(plan, (source * inverse_one * attention_gain).astype(BF))
    qkv_w = place_rows(
        plan,
        exchange_pieces(plan, column_piece([query_weight, key_weight, value_weight], parts, HD)),
    )
    normed = gather_close(plan, after(opened, (tables, qkv_w)))
    o_found = exchange_pieces(plan, row_piece(after(output_weight, normed[0]), parts))
    normed = flat(normed)

    wide = query_weight.shape[1] // parts
    share = max(1, HD * parts // key_weight.shape[1])
    narrow = key_weight.shape[1] * share // parts
    half_shape = (slots, parts // 2, rows, -1)
    projected = [matmul(item, qkv_w).reshape(half_shape) for item in normed]
    pair_piece = column_piece([gate_weight, up_weight], parts)
    shared = shared_pieces(plan, [gate_weight, up_weight], projected[1])
    rotated, attended, stats = attention_forward(projected, tables, order, slot_lengths)
    attended = flat(attended)
    attended, o_found, shared = after((attended, o_found, shared), rotated)
    o_w = place_columns(plan, o_found)
    opened = scatter_open(plan, attended, o_w, slots)
    hidden = source + scatter_close(plan, opened)

    inverse_two = lax.rsqrt(feature_total(hidden * hidden) / width + EPS)
    opened = gather_open(plan, (hidden * inverse_two * feedforward_gain).astype(BF))
    pair_w = shared_close(plan, shared, pair_piece, hidden)
    opened, pair_arrays = after((opened, [item for item, _ in pair_w]), hidden)
    pair_w = [(item, index) for item, (_, index) in zip(pair_arrays, pair_w)]
    normed_two = flat(gather_close(plan, opened))
    down_found = exchange_pieces(plan, row_piece(after(down_weight, normed_two[0]), parts))
    target_open = aside_open(plan, after(cotangent, normed_two[0]))
    units = gate_weight.shape[1] // parts
    masks = jnp.arange(parts, dtype=jnp.int32)
    places = plan.ordered(plan.place ^ masks, parts)
    active_here, *slopes_here = forward_units(places, normed_two[0], pair_w)
    away, target_open = after((normed_two[1], target_open), active_here)
    normed_two = (normed_two[0], away)
    target_open = aside_turn(plan, target_open)
    active_away, *slopes_away = forward_units(places, normed_two[1], pair_w)
    active = (active_here, active_away)
    active, target_open, down_found[:3] = after((active, target_open, down_found[:3]), active_away)
    target_all = flat(gather_close(plan, target_open, [scaled(0), scaled(1)]))
    target_all, down_found[3:] = after((target_all, down_found[3:]), active)
    down_sum = weight_gradient(plan, active, target_all, False)
    down_part = reduce_groups(down_sum)

    target = cotangent.astype(jnp.float32) * own_valid[:, :, None] * scale[:, None, None]
    target_away = after(target_all[1], down_sum)
    grads_away, away = backward_units(places, target_away, slopes_away, pair_w, down_found)
    target_here = after(target_all[0], away)
    grads_here, here = backward_units(places, target_here, slopes_here, pair_w, down_found)
    grad_pair = (grads_here, grads_away)
    opened = scatter_halves(plan, here, away, slots)
    grad_late = after(grad_pair, opened[-1])
    gate_sum = weight_gradient(plan, normed_two, grad_late, True, 0, 2)
    gate_part = reduce_groups(gate_sum)
    dn = scatter_close(plan, opened, (gate_sum, down_part))
    weighted = dn * feedforward_gain
    total_two = feature_total(weighted * hidden)
    grad_hidden = target + inverse_two * weighted - hidden * inverse_two**3 * total_two / width
    gain_two_sum = jnp.sum(dn * hidden * inverse_two, axis=(0, 1))

    down_w = place_columns(plan, after(down_found, dn))
    result_open = scatter_open(plan, after(active, grad_hidden), down_w, slots)
    up_sum = weight_gradient(plan, normed_two, after(grad_pair, grad_hidden), True, 1, 2)
    up_part = reduce_groups(up_sum)
    opened = after(gather_open(plan, grad_hidden.astype(BF)), (result_open, up_sum, gate_part))
    grad_hidden_all = flat(gather_close(plan, opened))
    result_open, down_part, gate_part = after((result_open, down_part, gate_part), grad_hidden_all)
    result_turned = scatter_turn(plan, result_open)
    down_sent = send_columns(plan, down_part)
    gate_sent = send_rows(plan, gate_part)
    grad_attended = [matmul(item, o_w.T).astype(BF) for item in grad_hidden_all]
    output_sum = weight_gradient(plan, attended, grad_hidden_all, False)
    grad_attended = after(grad_attended, output_sum)
    grad_attended = [item.reshape(half_shape) for item in grad_attended]
    back = attention_backward(rotated, grad_attended, stats, tables, order, slot_lengths)
    sent = (result_turned, down_sent, gate_sent, output_sum)
    back, sent = after((flat(back), sent), back)
    result_turned, down_sent, gate_sent, output_sum = sent
    opened = scatter_open(plan, back, qkv_w.T, slots)
    qkv_sum = weight_gradient(plan, normed, after(back, opened[-1]), True)
    result = hidden + scatter_end(plan, result_turned)
    outputs = jnp.where(own_valid[:, :, None], result, 0.0).astype(BF)
    output_part, qkv_part = reduce_both(plan, output_sum, qkv_sum)
    dm = scatter_close(plan, opened, (qkv_sum, up_part, outputs))
    up_part = after(up_part, dm)
    up_sent = send_rows(plan, up_part)
    flip = plan.side * (width // 2) if plan.fast else 0
    halves = jnp.sum(
        jnp.roll(qkv_sum.reshape(width, -1).astype(jnp.float32), flip, 0)
        * qkv_w.astype(jnp.float32),
        axis=1,
    )
    if plan.fast:
        gain_one_sum = halves[:half_width] + after(swap(halves[half_width:], "tensor", 1), dm)
    else:
        gain_one_sum = lax.psum_scatter(halves, "tensor", scatter_dimension=0, tiled=True)
    gain_one_sum = gain_one_sum / attention_gain
    weighted = dm * attention_gain
    total_one = feature_total(weighted * source)
    input_grad = grad_hidden + inverse_one * weighted - source * inverse_one**3 * total_one / width

    gains = total_over(total_over(jnp.stack([gain_one_sum, gain_two_sum]), "ctx"), "dp")
    output_part, qkv_part = after((output_part, qkv_part), gains)
    output_sent = send_columns(plan, output_part)
    qkv_sent = send_rows(plan, qkv_part)
    down_out = finish_rows(plan, down_sent)
    (gate_out,) = finish_columns(plan, gate_sent, ((units, 1),))
    (up_out,) = finish_columns(plan, up_sent, ((units, 1),))
    output_out = finish_rows(plan, output_sent)
    query_out, key_out, value_out = finish_columns(
        plan, qkv_sent, ((wide, 1), (narrow, share), (narrow, share))
    )
    return (
        outputs,
        input_grad.astype(BF),
        query_out,
        key_out,
        value_out,
        output_out,
        gate_out,
        up_out,
        down_out,
        gains[0],
        gains[1],
    )


def solution(mesh):
    return jax.shard_map(
        per_device,
        mesh=mesh,
        in_specs=(
            P("dp", "ctx", "tensor"),
            P("dp", "ctx", "tensor"),
            P(),
            P(),
            P("ctx", "tensor"),
            P("ctx", "tensor"),
            P("ctx", "tensor"),
            P("tensor", "ctx"),
            P("ctx", "tensor"),
            P("ctx", "tensor"),
            P("tensor", "ctx"),
            P("tensor"),
            P("tensor"),
        ),
        out_specs=(
            P("dp", "ctx", "tensor"),
            P("dp", "ctx", "tensor"),
            P(("dp", "ctx"), "tensor"),
            P(("dp", "ctx"), "tensor"),
            P(("dp", "ctx"), "tensor"),
            P("tensor", ("dp", "ctx")),
            P(("dp", "ctx"), "tensor"),
            P(("dp", "ctx"), "tensor"),
            P("tensor", ("dp", "ctx")),
            P("tensor"),
            P("tensor"),
        ),
        check_vma=False,
    )
```
